256 devices in a mesh: dp: 16 (over x, y), cent: 16 (over z, core).
Axes of the slice: x: 4, y: 4, z: 8, core: 2. Of those that a mesh axis runs over, the one named last changes fastest.
Arguments:
- embeddings: bfloat16 [32768, 1024], P('dp')
- centroids: bfloat16 [8192, 1024], P('cent')
- col_start: float32 [8192], P('cent'), may hold values from -6 to 6
Outputs:
- new_centroids: bfloat16 [8192, 1024], P('cent')
- row_potential: float32 [32768], P('dp')
- col_potential: float32 [8192], P('cent')
The draws below stay inside these ranges and needn't reach their ends.
All inputs are finite; a program needn't handle non-finite values.
Results may differ from the reference program's by a relative error of at most 0.0048.
Values may be sent and summed in bfloat16 or wider, within the bound.
A program may use at most 64 MiB of HBM per device.

```python
import math
import jax
import jax.numpy as jnp
from jax import lax

D = 1024
ROWS_DEV = 2048
ITERS = 3
N = 32768
K = 8192
N_DP = 16


def centre_base(key):
    return jax.random.normal(key, (K, D), jnp.float32)


def draw_centroids(key, part):
    base = centre_base(key)
    return base.astype(jnp.bfloat16)


def draw_embeddings(key, part):
    base = centre_base(key)
    key = jax.random.fold_in(key, 5)
    key_main, key_first, key_second, key_scale, key_noise, key_apart = jax.random.split(key, 6)
    index = jnp.arange(N)
    first = jax.random.randint(key_first, (N,), 0, K)
    second = (first + 1 + jax.random.randint(key_second, (N,), 0, K - 1)) % K
    kind = index // 64 % 3
    chosen = index % 64 == 0
    strength = jnp.exp(jax.random.uniform(key_scale, (N,), jnp.float32, jnp.log(200.0), jnp.log(600.0)))
    noise = jax.random.normal(key_noise, (N, D), jnp.float32)
    apart = jax.random.normal(key_apart, (N, D), jnp.float32)
    between = 0.5 * (base[first] + base[second]) + 0.3 * noise
    single = base[first] + 0.3 * noise
    shape_rows = jnp.where((kind == 0)[:, None], between, jnp.where((kind == 1)[:, None], single, apart))
    aligned = (strength / jnp.sqrt(1.0 * D))[:, None] * shape_rows
    drawn = jax.random.normal(key_main, (N, D), jnp.float32)
    values = jnp.where(chosen[:, None], aligned, drawn)
    return values.astype(jnp.bfloat16)


def levels(key, extent, cuts, least, top_value):
    def one(axis_at, parts):
        heights = jax.random.uniform(jax.random.fold_in(jax.random.fold_in(key, 6), axis_at), (parts,), jnp.float32, least / len(cuts), top_value / len(cuts))
        return jnp.repeat(jnp.exp(heights), extent[axis_at] // parts).reshape((-1,) + (1,) * (len(extent) - axis_at - 1))

    gain = one(*cuts[0])
    for cut in cuts[1:]:
        gain = gain * one(*cut)
    return gain


def normal_values(stream_key, extent, deviation, bound, pieces=(), dtype=jnp.bfloat16):
    array = jax.random.normal(stream_key, extent, jnp.float32) * deviation
    if len(pieces) > 0:
        array = levels(stream_key, extent, pieces, -0.22, 0.18) * array
    return jnp.clip(array, min=-bound, max=bound).astype(dtype)


def setup_inputs(seed: int = 0) -> dict:
    key_of = jax.random.split(jax.random.key(seed), 4)
    embeddings = draw_embeddings(jax.random.fold_in(key_of[3], 71), 0)
    centroids = draw_centroids(jax.random.fold_in(key_of[3], 71), 0)
    col_start = normal_values(key_of[2], (K,), 1.5, 6.0, ((0, 16),), jnp.float32)
    return {"embeddings": embeddings, "centroids": centroids, "col_start": col_start}


def tile(block, centroids):
    product = lax.dot_general(block, centroids, (((1,), (1,)), ((), ())), preferred_element_type=jnp.float32)
    return product * (1.0 / math.sqrt(D))

def sweep(blocks, centroids, col_now, n_total, k_total):

    def step(carry, block):
        col_peak, col_mass = carry
        scores = tile(block, centroids)
        shifted = scores + col_now[None, :]
        peak = lax.optimization_barrier(jnp.max(shifted, axis=1))
        mass = lax.optimization_barrier(jnp.sum(jnp.exp(shifted - peak[:, None]), axis=1))
        row_new = -jnp.log(n_total) - (peak + jnp.log(mass))
        lifted = scores + row_new[:, None]
        block_peak = lax.optimization_barrier(jnp.max(lifted, axis=0))
        block_mass = lax.optimization_barrier(jnp.sum(jnp.exp(lifted - block_peak[None, :]), axis=0))
        joined = jnp.maximum(col_peak, block_peak)
        total = col_mass * jnp.exp(col_peak - joined) + block_mass * jnp.exp(block_peak - joined)
        return ((joined, total), row_new)
    start = (jnp.full((centroids.shape[0],), -jnp.inf, jnp.float32), jnp.zeros((centroids.shape[0],), jnp.float32))
    (col_peak, col_mass), rows = lax.scan(step, start, blocks)
    col_new = -jnp.log(k_total) - (col_peak + jnp.log(col_mass))
    return (rows, col_new)

def reference(embeddings, centroids, col_start):
    n_total = float(embeddings.shape[0])
    k_total = float(centroids.shape[0])
    blocks = embeddings.reshape(N_DP, ROWS_DEV, D)
    col_now = col_start
    rows = None
    for step_index in range(ITERS):
        rows, col_now = sweep(blocks, centroids, col_now, n_total, k_total)

    def gather_step(acc, pair):
        block, row_block = pair
        scores = tile(block, centroids)
        plan = jnp.exp(scores + row_block[:, None] + col_now[None, :]).astype(jnp.bfloat16)
        acc = acc + lax.dot_general(plan, block, (((0,), (0,)), ((), ())), preferred_element_type=jnp.float32)
        return (acc, 0)
    acc, unused = lax.scan(gather_step, jnp.zeros((centroids.shape[0], D), jnp.float32), (blocks, rows))
    new_centroids = (acc * k_total).astype(jnp.bfloat16)
    return (new_centroids, rows.reshape(-1), col_now)
```

```python
import functools
import math

import jax
import jax.numpy as jnp
from jax import lax
from jax.experimental import pallas as pl
from jax.experimental.pallas import tpu as pltpu
from jax.sharding import PartitionSpec as P

MESH = pl.DeviceIdType.MESH
LOG2E = math.log2(math.e)
LN2 = math.log(2.0)
L = 128
BLK = 256
SUB = 32


def diag_mask():
    return lax.broadcasted_iota(jnp.int32, (L, L), 0) == lax.broadcasted_iota(jnp.int32, (L, L), 1)


def to_column(row):
    spread = jnp.where(diag_mask(), jnp.broadcast_to(row, (L, L)), 0.0)
    return jnp.broadcast_to(jnp.sum(spread, axis=1, keepdims=True), (L, L))


def to_row(column):
    return jnp.sum(jnp.where(diag_mask(), column, 0.0), axis=0, keepdims=True)


def kernel(
    nd, nc, side, n_total, k_total,
    g_ref, c_hbm, e_hbm,
    out_hbm, rp_ref, cp_ref,
    cv, ev, tm, am, bm, gcol, col1, col2, rrow, crow,
    l_all, rho2, rho3, lc_all, cs2, cs3,
    p1s, p1r, p2s, p2r, p3s,
    load_sem, barrier_unused, rs_sem, rr_sem, cs_sem, cr_sem,
    b1s_sem, b1r_sem, b2s_sem, b2r_sem, b3s_sem, b3r_sem, own_sem,
):
    kc, d = cv.shape
    nk = tm.shape[0]
    nb = nk * L // BLK
    nj = kc // L
    dp = lax.axis_index("dp")
    ce = lax.axis_index("cent")
    x, y = dp // side, lax.rem(dp, side)

    barrier = pltpu.get_barrier_semaphore()

    def greet_cent(k, c):
        pl.semaphore_signal(barrier, inc=1, device_id=(dp, lax.rem(ce + k, nc)), device_id_type=MESH)
        return c

    def greet_dp(k, c):
        pl.semaphore_signal(barrier, inc=1, device_id=(lax.rem(dp + k, nd), ce), device_id_type=MESH)
        return c

    lax.fori_loop(1, nc, greet_cent, 0)
    lax.fori_loop(1, nd, greet_dp, 0)

    c_load = pltpu.make_async_copy(c_hbm, cv, load_sem.at[nb])
    c_load.start()

    def e_load(b):
        rows = pl.ds(b * BLK, BLK)
        return pltpu.make_async_copy(e_hbm.at[rows], ev.at[rows], load_sem.at[b])

    for b in range(nb):
        e_load(b).start()

    for t in range(nj):
        gcol[pl.ds(t * L, L), :] = to_column(g_ref[pl.ds(t, 1), :] * LOG2E)
    c_load.wait()

    scale = LOG2E / math.sqrt(d)

    def score_block(b, carry):
        e_load(b).wait()
        block = ev[pl.ds(pl.multiple_of(b * BLK, BLK), BLK), :]
        product = lax.dot_general(cv[...], block, (((1,), (1,)), ((), ())), preferred_element_type=jnp.float32)
        product = product * scale
        for h in range(BLK // L):
            tm[b * (BLK // L) + h] = product[:, h * L : (h + 1) * L]
        for h in range(BLK // L):
            k = b * (BLK // L) + h
            peak = jnp.max(tm[k] + gcol[...], axis=0, keepdims=True)
            mass = jnp.sum(jnp.exp2(tm[k] + gcol[...] - peak), axis=0, keepdims=True)
            l_all[ce, pl.ds(k, 1), :] = peak + jnp.log2(mass)
        return carry

    lax.fori_loop(0, nb, score_block, 0)
    pl.semaphore_wait(barrier, nc - 1 + nd - 1)

    def cent_copy(phase, buf, k):
        to = lax.rem(ce + k, nc)
        return pltpu.make_async_remote_copy(
            src_ref=buf.at[ce], dst_ref=buf.at[ce],
            send_sem=rs_sem.at[phase, to], recv_sem=rr_sem.at[phase, ce],
            device_id=(dp, to), device_id_type=MESH,
        )

    def cent_arrival(phase, buf, k):
        fr = lax.rem(ce + k, nc)
        return pltpu.make_async_remote_copy(
            src_ref=buf.at[fr], dst_ref=buf.at[fr],
            send_sem=rs_sem.at[phase, fr], recv_sem=rr_sem.at[phase, fr],
            device_id=(dp, fr), device_id_type=MESH,
        )

    def dp_copy(phase, buf, k):
        to = lax.rem(dp + k, nd)
        return pltpu.make_async_remote_copy(
            src_ref=buf.at[dp], dst_ref=buf.at[dp],
            send_sem=cs_sem.at[phase, to], recv_sem=cr_sem.at[phase, dp],
            device_id=(to, ce), device_id_type=MESH,
        )

    def dp_arrival(phase, buf, k):
        fr = lax.rem(dp + k, nd)
        return pltpu.make_async_remote_copy(
            src_ref=buf.at[fr], dst_ref=buf.at[fr],
            send_sem=cs_sem.at[phase, fr], recv_sem=cr_sem.at[phase, fr],
            device_id=(fr, ce), device_id_type=MESH,
        )

    def loop(n, act):
        def step(k, c):
            act(k)
            return c

        lax.fori_loop(1, n, step, 0)

    def cent_exchange(phase, buf):
        loop(nc, lambda k: cent_copy(phase, buf, k).start())
        loop(nc, lambda k: cent_arrival(phase, buf, k).wait_recv())

    def dp_start(phase, buf):
        loop(nd, lambda k: dp_copy(phase, buf, k).start())

    def dp_finish(phase, buf):
        loop(nd, lambda k: dp_arrival(phase, buf, k).wait_recv())

    def joined(buf, n):
        peak = buf[0]
        for s in range(1, n):
            peak = jnp.maximum(peak, buf[s])
        total = jnp.exp2(buf[0] - peak)
        for s in range(1, n):
            total = total + jnp.exp2(buf[s] - peak)
        return peak + jnp.log2(total)

    def added(buf, n):
        total = buf[0].astype(jnp.float32)
        for s in range(1, n):
            total = total + buf[s].astype(jnp.float32)
        return total

    cent_exchange(0, l_all)
    rrow[...] = -math.log2(n_total) - joined(l_all, nc)

    def first_columns(jb, carry):
        rows = pl.ds(pl.multiple_of(jb * SUB, SUB), SUB)
        peak = tm[0, rows, :] + rrow[pl.ds(0, 1), :]
        for k in range(1, nk):
            peak = jnp.maximum(peak, tm[k, rows, :] + rrow[pl.ds(k, 1), :])
        peak = jnp.broadcast_to(jnp.max(peak, axis=1, keepdims=True), (SUB, L))
        mass = jnp.zeros((SUB, L), jnp.float32)
        for k in range(nk):
            value = jnp.exp2(tm[k, rows, :] + rrow[pl.ds(k, 1), :] - peak)
            am[k, rows, :] = value
            mass = mass + value
        col1[rows, :] = peak
        col2[rows, :] = jnp.broadcast_to(jnp.sum(mass, axis=1, keepdims=True), (SUB, L))
        return carry

    lax.fori_loop(0, kc // SUB, first_columns, 0)
    for t in range(nj):
        top = to_row(col1[pl.ds(t * L, L), :])
        crow[pl.ds(t, 1), :] = top
        lc_all[dp, pl.ds(t, 1), :] = top + jnp.log2(to_row(col2[pl.ds(t * L, L), :]))
    dp_start(0, lc_all)
    dp_finish(0, lc_all)
    g_one = -math.log2(k_total) - joined(lc_all, nd)
    lift = jnp.exp2(crow[...] + g_one)
    crow[...] = g_one
    for t in range(nj):
        col1[pl.ds(t * L, L), :] = to_column(lift[t : t + 1, :])

    def second_rows(k, carry):
        value = am[k] * col1[...]
        am[k] = value
        rho2[ce, pl.ds(k, 1), :] = jnp.sum(value, axis=0, keepdims=True)
        return carry

    lax.fori_loop(0, nk, second_rows, 0)
    cent_exchange(1, rho2)
    u_two = 1.0 / (n_total * added(rho2, nc))
    bm_rows = rrow

    def column_sums(u, target, keep):
        def body(jb, carry):
            rows = pl.ds(pl.multiple_of(jb * SUB, SUB), SUB)
            mass = jnp.zeros((SUB, L), jnp.float32)
            for k in range(nk):
                value = am[k, rows, :] * u[k : k + 1, :]
                if keep:
                    bm[rows, k * L : (k + 1) * L] = value.astype(jnp.bfloat16)
                mass = mass + value
            col2[rows, :] = jnp.broadcast_to(jnp.sum(mass, axis=1, keepdims=True), (SUB, L))
            return carry

        lax.fori_loop(0, kc // SUB, body, 0)
        for t in range(nj):
            target[dp, pl.ds(t, 1), :] = to_row(col2[pl.ds(t * L, L), :])

    column_sums(u_two, cs2, False)
    dp_start(1, cs2)
    dp_finish(1, cs2)
    v_two = 1.0 / (k_total * added(cs2, nd))
    for t in range(nj):
        col1[pl.ds(t * L, L), :] = to_column(v_two[t : t + 1, :])

    def third_rows(k, carry):
        rho3[ce, pl.ds(k, 1), :] = jnp.sum(am[k] * col1[...], axis=0, keepdims=True)
        return carry

    lax.fori_loop(0, nk, third_rows, 0)
    cent_exchange(2, rho3)
    u_three = 1.0 / (n_total * added(rho3, nc))
    rp_ref[...] = (bm_rows[...] + jnp.log2(u_three)) * LN2

    column_sums(u_three, cs3, True)
    dp_start(2, cs3)

    hr = kc // 2
    dq = d // side
    here = (x, y)

    def along(h, stage, i):
        if (h + stage) % 2 == 0:
            return (i * side + y, ce)
        return (x * side + i, ce)

    def place(h, stage):
        return here[(h + stage) % 2]

    def b1_copy(h, i):
        me = place(h, 0)
        return pltpu.make_async_remote_copy(
            src_ref=p1s.at[h, i], dst_ref=p1r.at[h, me],
            send_sem=b1s_sem.at[h, i], recv_sem=b1r_sem.at[h, me],
            device_id=along(h, 0, i), device_id_type=MESH,
        )

    def b1_arrival(h, i):
        return pltpu.make_async_remote_copy(
            src_ref=p1s.at[h, i], dst_ref=p1r.at[h, i],
            send_sem=b1s_sem.at[h, i], recv_sem=b1r_sem.at[h, i],
            device_id=along(h, 0, i), device_id_type=MESH,
        )

    def b2_copy(h, i):
        me = place(h, 1)
        return pltpu.make_async_remote_copy(
            src_ref=p2r.at[h, me], dst_ref=p2r.at[h, me],
            send_sem=b2s_sem.at[h, i], recv_sem=b2r_sem.at[h, me],
            device_id=along(h, 1, i), device_id_type=MESH,
        )

    def b2_arrival(h, i):
        return pltpu.make_async_remote_copy(
            src_ref=p2r.at[h, i], dst_ref=p2r.at[h, i],
            send_sem=b2s_sem.at[h, i], recv_sem=b2r_sem.at[h, i],
            device_id=along(h, 1, i), device_id_type=MESH,
        )

    def out_part(h, i):
        return out_hbm.at[pl.ds(h * hr, hr), pl.ds(pl.multiple_of(i * dq, L), dq)]

    def b3_copy(h, i):
        me = place(h, 0)
        return pltpu.make_async_remote_copy(
            src_ref=p3s.at[h], dst_ref=out_part(h, me),
            send_sem=b3s_sem.at[h, i], recv_sem=b3r_sem.at[h, me],
            device_id=along(h, 0, i), device_id_type=MESH,
        )

    def b3_arrival(h, i):
        return pltpu.make_async_remote_copy(
            src_ref=p3s.at[h], dst_ref=out_part(h, i),
            send_sem=b3s_sem.at[h, i], recv_sem=b3r_sem.at[h, i],
            device_id=along(h, 0, i), device_id_type=MESH,
        )

    def partial_block(step, carry):
        for h in range(2):
            i = lax.rem(place(h, 0) + 1 + step, side)
            cols = pl.ds(pl.multiple_of(i * dq, L), dq)
            block = jnp.dot(bm[pl.ds(h * hr, hr), :], ev[:, cols], preferred_element_type=jnp.float32)
            block = block.astype(jnp.bfloat16)

            @pl.when(step < side - 1)
            def _():
                p1s[h, i] = block
                b1_copy(h, i).start()

            @pl.when(step == side - 1)
            def _():
                p1r[h, i] = block

        return carry

    lax.fori_loop(0, side, partial_block, 0)

    for h in range(2):
        me = place(h, 0)
        loop(side, lambda k: b1_arrival(h, lax.rem(me + k, side)).wait_recv())
        p2r[h, place(h, 1)] = added(p1r.at[h], side).astype(jnp.bfloat16)
        mine = place(h, 1)
        loop(side, lambda k: b2_copy(h, lax.rem(mine + k, side)).start())

    dp_finish(2, cs3)
    total = added(cs3, nd)
    cp_ref[...] = (crow[...] - jnp.log2(k_total * total)) * LN2
    back = 1.0 / total
    for t in range(nj):
        col1[pl.ds(t * L, L), :] = to_column(back[t : t + 1, :])

    own = []
    for h in range(2):
        me = place(h, 0)
        mine = place(h, 1)
        loop(side, lambda k: b2_arrival(h, lax.rem(mine + k, side)).wait_recv())
        whole = added(p2r.at[h], side)
        factor = col1[pl.ds(h * hr, hr), :]
        for q in range(dq // L):
            p3s[h, :, q * L : (q + 1) * L] = (whole[:, q * L : (q + 1) * L] * factor).astype(jnp.bfloat16)
        loop(side, lambda k: b3_copy(h, lax.rem(me + k, side)).start())
        keep = pltpu.make_async_copy(p3s.at[h], out_part(h, me), own_sem.at[h])
        keep.start()
        own.append(keep)
    for h in range(2):
        me = place(h, 0)
        loop(side, lambda k: b3_arrival(h, lax.rem(me + k, side)).wait_recv())
        own[h].wait()

    for phase, buf in enumerate((l_all, rho2, rho3)):
        loop(nc, lambda k: cent_copy(phase, buf, k).wait_send())
    for phase, buf in enumerate((lc_all, cs2, cs3)):
        loop(nd, lambda k: dp_copy(phase, buf, k).wait_send())
    for h in range(2):
        me = place(h, 0)
        mine = place(h, 1)
        loop(side, lambda k: b1_copy(h, lax.rem(me + k, side)).wait_send())
        loop(side, lambda k: b2_copy(h, lax.rem(mine + k, side)).wait_send())
        loop(side, lambda k: b3_copy(h, lax.rem(me + k, side)).wait_send())


def on_device(nd, nc, embeddings, centroids, col_start):
    rows, d = embeddings.shape
    kc = centroids.shape[0]
    side = math.isqrt(nd)
    nk, nj = rows // L, kc // L
    hr, dq = kc // 2, d // side
    f32, bf16 = jnp.float32, jnp.bfloat16
    dma = pltpu.SemaphoreType.DMA
    vmem = pl.BlockSpec(memory_space=pltpu.VMEM)
    anywhere = pl.BlockSpec(memory_space=pl.ANY)
    out, row_potential, col_potential = pl.pallas_call(
        functools.partial(kernel, nd, nc, side, float(rows * nd), float(kc * nc)),
        out_shape=(
            jax.ShapeDtypeStruct((kc, d), bf16),
            jax.ShapeDtypeStruct((nk, L), f32),
            jax.ShapeDtypeStruct((nj, L), f32),
        ),
        in_specs=[vmem, anywhere, anywhere],
        out_specs=(anywhere, vmem, vmem),
        scratch_shapes=[
            pltpu.VMEM((kc, d), bf16),
            pltpu.VMEM((rows, d), bf16),
            pltpu.VMEM((nk, kc, L), f32),
            pltpu.VMEM((nk, kc, L), f32),
            pltpu.VMEM((kc, rows), bf16),
            pltpu.VMEM((kc, L), f32),
            pltpu.VMEM((kc, L), f32),
            pltpu.VMEM((kc, L), f32),
            pltpu.VMEM((nk, L), f32),
            pltpu.VMEM((nj, L), f32),
            pltpu.VMEM((nc, nk, L), f32),
            pltpu.VMEM((nc, nk, L), f32),
            pltpu.VMEM((nc, nk, L), f32),
            pltpu.VMEM((nd, nj, L), f32),
            pltpu.VMEM((nd, nj, L), f32),
            pltpu.VMEM((nd, nj, L), f32),
            pltpu.VMEM((2, side, hr, dq), bf16),
            pltpu.VMEM((2, side, hr, dq), bf16),
            pltpu.VMEM((2, hr, dq), bf16),
            pltpu.VMEM((2, side, hr, dq), bf16),
            pltpu.VMEM((2, hr, dq), bf16),
            dma((rows // BLK + 1,)),
            dma((1,)),
            dma((3, nc)),
            dma((3, nc)),
            dma((3, nd)),
            dma((3, nd)),
            dma((2, side)),
            dma((2, side)),
            dma((2, side)),
            dma((2, side)),
            dma((2, side)),
            dma((2, side)),
            dma((2,)),
        ],
        compiler_params=pltpu.CompilerParams(
            collective_id=0, has_side_effects=True, vmem_limit_bytes=56 * 2**20
        ),
        cost_estimate=pl.CostEstimate(
            flops=4 * rows * kc * d, bytes_accessed=2 * (rows + 2 * kc) * d, transcendentals=2 * rows * kc
        ),
        name="sinkhorn",
    )(col_start.reshape(nj, L), centroids, embeddings)
    return out, row_potential.reshape(rows), col_potential.reshape(kc)


def solution(mesh):
    return jax.shard_map(
        functools.partial(on_device, mesh.shape["dp"], mesh.shape["cent"]),
        mesh=mesh,
        in_specs=(P("dp", None), P("cent", None), P("cent")),
        out_specs=(P("cent", None), P("dp"), P("cent")),
        check_vma=False,
    )
```

```python
import functools
import math

import jax
import jax.numpy as jnp
from jax import lax
from jax.experimental import pallas as pl
from jax.experimental.pallas import tpu as pltpu
from jax.sharding import PartitionSpec as P

MESH = pl.DeviceIdType.MESH
LOG2E = math.log2(math.e)
LN2 = math.log(2.0)
L = 128
BLK = 256
SUB = 32
CHUNKS = 2


def diag_mask():
    return lax.broadcasted_iota(jnp.int32, (L, L), 0) == lax.broadcasted_iota(jnp.int32, (L, L), 1)


def to_column(row):
    spread = jnp.where(diag_mask(), jnp.broadcast_to(row, (L, L)), 0.0)
    return jnp.broadcast_to(jnp.sum(spread, axis=1, keepdims=True), (L, L))


def to_row(column):
    return jnp.sum(jnp.where(diag_mask(), column, 0.0), axis=0, keepdims=True)


def kernel(
    nd, nc, side, n_total, k_total,
    g_ref, c_hbm, e_hbm,
    out_hbm, rp_ref, cp_ref,
    cv, ev, tm, am, bm, gcol, col1, col2, rrow, crow, rsum,
    l_all, rho2, rho3, lc_all, cs2, cs3,
    p1s, p1r, p2r, p3s,
    load_sem, rs_sem, rr_sem, cs_sem, cr_sem,
    b1s_sem, b1r_sem, b2s_sem, b2r_sem, b3s_sem, b3r_sem, own_sem,
):
    kc, d = cv.shape
    nk = tm.shape[0]
    nb = nk * L // BLK
    nj = kc // L
    dp = lax.axis_index("dp")
    ce = lax.axis_index("cent")
    x, y = dp // side, lax.rem(dp, side)

    cent_offsets = sorted(
        ((dz, dc) for dz in range(nc // 2) for dc in range(2) if dz or dc),
        key=lambda o: (-min(o[0], nc // 2 - o[0]), o),
    )
    dp_offsets = sorted(
        ((dx, dy) for dx in range(side) for dy in range(side) if dx or dy),
        key=lambda o: (-min(o[0], side - o[0]) - min(o[1], side - o[1]), o),
    )
    z, core = ce // 2, lax.rem(ce, 2)

    def cent_at(o, sign):
        return lax.rem(z + sign * o[0] + nc // 2, nc // 2) * 2 + lax.rem(core + o[1], 2)

    def dp_at(o, sign):
        return lax.rem(x + sign * o[0] + side, side) * side + lax.rem(y + sign * o[1] + side, side)

    c_load = pltpu.make_async_copy(c_hbm, cv, load_sem.at[nb])
    c_load.start()

    def e_load(b):
        rows = pl.ds(b * BLK, BLK)
        return pltpu.make_async_copy(e_hbm.at[rows], ev.at[rows], load_sem.at[b])

    for b in range(nb):
        e_load(b).start()

    barrier = pltpu.get_barrier_semaphore()
    for o in cent_offsets:
        pl.semaphore_signal(barrier, inc=1, device_id=(dp, cent_at(o, 1)), device_id_type=MESH)
    for o in dp_offsets:
        pl.semaphore_signal(barrier, inc=1, device_id=(dp_at(o, 1), ce), device_id_type=MESH)

    for t in range(nj):
        gcol[pl.ds(t * L, L), :] = to_column(g_ref[pl.ds(t, 1), :] * LOG2E)
    c_load.wait()

    scale = LOG2E / math.sqrt(d)

    def score_block(b, carry):
        e_load(b).wait()
        block = ev[pl.ds(pl.multiple_of(b * BLK, BLK), BLK), :]
        product = lax.dot_general(cv[...], block, (((1,), (1,)), ((), ())), preferred_element_type=jnp.float32)
        product = product * scale
        for h in range(BLK // L):
            tm[b * (BLK // L) + h] = product[:, h * L : (h + 1) * L]
        for h in range(BLK // L):
            k = b * (BLK // L) + h
            peak = jnp.max(tm[k] + gcol[...], axis=0, keepdims=True)
            mass = jnp.sum(jnp.exp2(tm[k] + gcol[...] - peak), axis=0, keepdims=True)
            l_all[ce, pl.ds(k, 1), :] = peak + jnp.log2(mass)
        return carry

    def cent_copy(phase, ref, k):
        return pltpu.make_async_remote_copy(
            src_ref=ref(ce), dst_ref=ref(ce),
            send_sem=rs_sem.at[phase, k], recv_sem=rr_sem.at[phase, k],
            device_id=(dp, cent_at(cent_offsets[k], 1)), device_id_type=MESH,
        )

    def cent_arrival(phase, ref, k):
        fr = cent_at(cent_offsets[k], -1)
        return pltpu.make_async_remote_copy(
            src_ref=ref(fr), dst_ref=ref(fr),
            send_sem=rs_sem.at[phase, k], recv_sem=rr_sem.at[phase, k],
            device_id=(dp, fr), device_id_type=MESH,
        )

    def dp_copy(phase, buf, k):
        return pltpu.make_async_remote_copy(
            src_ref=buf.at[dp], dst_ref=buf.at[dp],
            send_sem=cs_sem.at[phase, k], recv_sem=cr_sem.at[phase, k],
            device_id=(dp_at(dp_offsets[k], 1), ce), device_id_type=MESH,
        )

    def dp_arrival(phase, buf, k):
        fr = dp_at(dp_offsets[k], -1)
        return pltpu.make_async_remote_copy(
            src_ref=buf.at[fr], dst_ref=buf.at[fr],
            send_sem=cs_sem.at[phase, k], recv_sem=cr_sem.at[phase, k],
            device_id=(fr, ce), device_id_type=MESH,
        )

    def cent_start(phase, ref):
        for k in range(nc - 1):
            cent_copy(phase, ref, k).start()

    def cent_finish(phase, ref):
        for k in reversed(range(nc - 1)):
            cent_arrival(phase, ref, k).wait_recv()

    def dp_start(phase, buf):
        for k in range(nd - 1):
            dp_copy(phase, buf, k).start()

    def dp_finish(phase, buf):
        for k in reversed(range(nd - 1)):
            dp_arrival(phase, buf, k).wait_recv()

    early = nk // 2
    part_a = pl.ds(0, early)
    part_b = pl.ds(early, nk - early)

    def l_part(part):
        return lambda s: l_all.at[s, part]

    def whole_of(buf):
        return lambda s: buf.at[s]

    def joined(buf, n):
        peak = buf[0]
        for s in range(1, n):
            peak = jnp.maximum(peak, buf[s])
        total = jnp.exp2(buf[0] - peak)
        for s in range(1, n):
            total = total + jnp.exp2(buf[s] - peak)
        return peak + jnp.log2(total)

    def added(buf, n):
        total = buf[0].astype(jnp.float32)
        for s in range(1, n):
            total = total + buf[s].astype(jnp.float32)
        return total

    lax.fori_loop(0, early * L // BLK, score_block, 0)
    pl.semaphore_wait(barrier, nc - 1 + nd - 1)
    cent_start(0, l_part(part_a))
    lax.fori_loop(early * L // BLK, nb, score_block, 0)
    cent_start(1, l_part(part_b))
    cent_finish(0, l_part(part_a))
    cent_finish(1, l_part(part_b))

    rrow[...] = -math.log2(n_total) - joined(l_all, nc)

    def first_columns(jb, carry):
        rows = pl.ds(pl.multiple_of(jb * SUB, SUB), SUB)
        peak = tm[0, rows, :] + rrow[pl.ds(0, 1), :]
        for k in range(1, nk):
            peak = jnp.maximum(peak, tm[k, rows, :] + rrow[pl.ds(k, 1), :])
        peak = jnp.broadcast_to(jnp.max(peak, axis=1, keepdims=True), (SUB, L))
        mass = jnp.zeros((SUB, L), jnp.float32)
        for k in range(nk):
            value = jnp.exp2(tm[k, rows, :] + rrow[pl.ds(k, 1), :] - peak)
            am[k, rows, :] = value
            mass = mass + value
        col1[rows, :] = peak
        col2[rows, :] = jnp.broadcast_to(jnp.sum(mass, axis=1, keepdims=True), (SUB, L))
        return carry

    lax.fori_loop(0, kc // SUB, first_columns, 0)
    for t in range(nj):
        top = to_row(col1[pl.ds(t * L, L), :])
        crow[pl.ds(t, 1), :] = top
        lc_all[dp, pl.ds(t, 1), :] = top + jnp.log2(to_row(col2[pl.ds(t * L, L), :]))
    dp_start(0, lc_all)
    dp_finish(0, lc_all)
    g_one = -math.log2(k_total) - joined(lc_all, nd)
    lift = jnp.exp2(crow[...] + g_one)
    crow[...] = g_one
    for t in range(nj):
        col1[pl.ds(t * L, L), :] = to_column(lift[t : t + 1, :])

    def second_rows(k, carry):
        value = am[k] * col1[...]
        am[k] = value
        rsum[pl.ds(k, 1), :] = jnp.sum(value, axis=0, keepdims=True)
        return carry

    lax.fori_loop(0, nk, second_rows, 0)
    rho2[ce] = rsum[...].astype(rho2.dtype)
    cent_start(2, whole_of(rho2))
    cent_finish(2, whole_of(rho2))
    u_two = 1.0 / (n_total * added(rho2, nc))

    def column_sums(u, target, keep):
        def body(jb, carry):
            rows = pl.ds(pl.multiple_of(jb * SUB, SUB), SUB)
            mass = jnp.zeros((SUB, L), jnp.float32)
            for k in range(nk):
                value = am[k, rows, :] * u[k : k + 1, :]
                if keep:
                    bm[rows, k * L : (k + 1) * L] = value.astype(jnp.bfloat16)
                mass = mass + value
            col2[rows, :] = jnp.broadcast_to(jnp.sum(mass, axis=1, keepdims=True), (SUB, L))
            return carry

        lax.fori_loop(0, kc // SUB, body, 0)
        for t in range(nj):
            target[dp, pl.ds(t, 1), :] = to_row(col2[pl.ds(t * L, L), :])

    column_sums(u_two, cs2, False)
    dp_start(1, cs2)
    dp_finish(1, cs2)
    v_two = 1.0 / (k_total * added(cs2, nd))
    for t in range(nj):
        col1[pl.ds(t * L, L), :] = to_column(v_two[t : t + 1, :])

    def third_rows(k, carry):
        rho3[ce, pl.ds(k, 1), :] = jnp.sum(am[k] * col1[...], axis=0, keepdims=True)
        return carry

    lax.fori_loop(0, nk, third_rows, 0)
    cent_start(3, whole_of(rho3))
    cent_finish(3, whole_of(rho3))
    u_three = 1.0 / (n_total * added(rho3, nc))
    rp_ref[...] = (rrow[...] + jnp.log2(u_three)) * LN2

    column_sums(u_three, cs3, True)
    dp_start(2, cs3)

    hr = kc // 2
    cr = hr // CHUNKS
    dq = d // side
    here = (x, y)
    offsets = sorted(range(1, side), key=lambda o: -min(o, side - o))

    def along(h, stage, i):
        if (h + stage) % 2 == 0:
            return (i * side + y, ce)
        return (x * side + i, ce)

    def place(h, stage, o=0):
        return lax.rem(here[(h + stage) % 2] + o + side, side)

    def chunk(c):
        return pl.ds(c * cr, cr)

    def b1(h, c, n, to, fr):
        return pltpu.make_async_remote_copy(
            src_ref=p1s.at[h, to, chunk(c)], dst_ref=p1r.at[h, fr, chunk(c)],
            send_sem=b1s_sem.at[h, c, n], recv_sem=b1r_sem.at[h, c, n],
            device_id=along(h, 0, to), device_id_type=MESH,
        )

    def b2(h, c, n, to, fr):
        return pltpu.make_async_remote_copy(
            src_ref=p2r.at[h, fr, chunk(c)], dst_ref=p2r.at[h, fr, chunk(c)],
            send_sem=b2s_sem.at[h, c, n], recv_sem=b2r_sem.at[h, c, n],
            device_id=along(h, 1, to), device_id_type=MESH,
        )

    def out_part(h, c, i):
        return out_hbm.at[pl.ds(h * hr + c * cr, cr), pl.ds(pl.multiple_of(i * dq, L), dq)]

    def b3(h, c, n, to, fr):
        return pltpu.make_async_remote_copy(
            src_ref=p3s.at[h, chunk(c)], dst_ref=out_part(h, c, fr),
            send_sem=b3s_sem.at[h, c, n], recv_sem=b3r_sem.at[h, c, n],
            device_id=along(h, 0, to), device_id_type=MESH,
        )

    def sending(copy, stage, h, c, n):
        return copy(h, c, n, place(h, stage, offsets[n]), place(h, stage))

    def arriving(copy, stage, h, c, n):
        return copy(h, c, n, place(h, stage), place(h, stage, -offsets[n]))

    def block_of(h, c, i):
        cols = pl.ds(pl.multiple_of(i * dq, L), dq)
        rows = pl.ds(h * hr + c * cr, cr)
        return jnp.dot(bm[rows, :], ev[:, cols], preferred_element_type=jnp.float32).astype(jnp.bfloat16)

    pieces = [(c, h) for c in range(CHUNKS) for h in range(2)]
    for c in range(CHUNKS):
        for n in range(side - 1):
            for h in range(2):
                p1s[h, place(h, 0, offsets[n]), chunk(c)] = block_of(h, c, place(h, 0, offsets[n]))
                sending(b1, 0, h, c, n).start()
        for h in range(2):
            p1r[h, place(h, 0), chunk(c)] = block_of(h, c, place(h, 0))

    def summed(buf, h, c):
        total = buf[h, 0, chunk(c)].astype(jnp.float32)
        for i in range(1, side):
            total = total + buf[h, i, chunk(c)].astype(jnp.float32)
        return total

    for c, h in pieces:
        for n in reversed(range(side - 1)):
            arriving(b1, 0, h, c, n).wait_recv()
        p2r[h, place(h, 1), chunk(c)] = summed(p1r, h, c).astype(jnp.bfloat16)
        for n in range(side - 1):
            sending(b2, 1, h, c, n).start()

    dp_finish(2, cs3)
    total = added(cs3, nd)
    cp_ref[...] = (crow[...] - jnp.log2(k_total * total)) * LN2
    back = 1.0 / total
    for t in range(nj):
        col1[pl.ds(t * L, L), :] = to_column(back[t : t + 1, :])

    own = []
    for c, h in pieces:
        for n in reversed(range(side - 1)):
            arriving(b2, 1, h, c, n).wait_recv()
        whole = summed(p2r, h, c)
        factor = col1[pl.ds(h * hr + c * cr, cr), :]
        for q in range(dq // L):
            p3s[h, chunk(c), q * L : (q + 1) * L] = (whole[:, q * L : (q + 1) * L] * factor).astype(jnp.bfloat16)
        for n in range(side - 1):
            sending(b3, 0, h, c, n).start()
        keep = pltpu.make_async_copy(p3s.at[h, chunk(c)], out_part(h, c, place(h, 0)), own_sem.at[h, c])
        keep.start()
        own.append(keep)

    for phase, ref in enumerate((l_part(part_a), l_part(part_b), whole_of(rho2), whole_of(rho3))):
        for k in range(nc - 1):
            cent_copy(phase, ref, k).wait_send()
    for phase, buf in enumerate((lc_all, cs2, cs3)):
        for k in range(nd - 1):
            dp_copy(phase, buf, k).wait_send()
    for c, h in pieces:
        for n in range(side - 1):
            sending(b1, 0, h, c, n).wait_send()
            sending(b2, 1, h, c, n).wait_send()
    for c, h in pieces:
        for n in reversed(range(side - 1)):
            arriving(b3, 0, h, c, n).wait_recv()
    for keep in own:
        keep.wait()
    for c, h in pieces:
        for n in range(side - 1):
            sending(b3, 0, h, c, n).wait_send()


def closing(c_in, r_in, k_in, c_out, r_out, k_out, c_v, r_v, k_v, in_sem, out_sem):
    step = c_v.shape[0] // 4
    parts = [(c_in.at[pl.ds(i * step, step)], c_v.at[pl.ds(i * step, step)], c_out.at[pl.ds(i * step, step)]) for i in range(4)]
    parts += [(r_in, r_v, r_out), (k_in, k_v, k_out)]
    arriving = [pltpu.make_async_copy(a, b, in_sem.at[i]) for i, (a, b, _) in enumerate(parts)]
    leaving = [pltpu.make_async_copy(b, c, out_sem.at[i]) for i, (_, b, c) in enumerate(parts)]
    for copy in arriving:
        copy.start()
    for a, b in zip(arriving, leaving):
        a.wait()
        b.start()
    for copy in leaving:
        copy.wait()


def on_device(nd, nc, embeddings, centroids, col_start):
    rows, d = embeddings.shape
    kc = centroids.shape[0]
    side = math.isqrt(nd)
    nk, nj = rows // L, kc // L
    hr, dq = kc // 2, d // side
    f32, bf16 = jnp.float32, jnp.bfloat16
    dma = pltpu.SemaphoreType.DMA
    vmem = pl.BlockSpec(memory_space=pltpu.VMEM)
    anywhere = pl.BlockSpec(memory_space=pl.ANY)
    out, row_potential, col_potential = pl.pallas_call(
        functools.partial(kernel, nd, nc, side, float(rows * nd), float(kc * nc)),
        out_shape=(
            jax.ShapeDtypeStruct((kc, d), bf16),
            jax.ShapeDtypeStruct((nk, L), f32),
            jax.ShapeDtypeStruct((nj, L), f32),
        ),
        in_specs=[vmem, anywhere, anywhere],
        out_specs=(anywhere, vmem, vmem),
        scratch_shapes=[
            pltpu.VMEM((kc, d), bf16),
            pltpu.VMEM((rows, d), bf16),
            pltpu.VMEM((nk, kc, L), f32),
            pltpu.VMEM((nk, kc, L), f32),
            pltpu.VMEM((kc, rows), bf16),
            pltpu.VMEM((kc, L), f32),
            pltpu.VMEM((kc, L), f32),
            pltpu.VMEM((kc, L), f32),
            pltpu.VMEM((nk, L), f32),
            pltpu.VMEM((nj, L), f32),
            pltpu.VMEM((nk, L), f32),
            pltpu.VMEM((nc, nk, L), f32),
            pltpu.VMEM((nc, nk, L), bf16),
            pltpu.VMEM((nc, nk, L), f32),
            pltpu.VMEM((nd, nj, L), f32),
            pltpu.VMEM((nd, nj, L), f32),
            pltpu.VMEM((nd, nj, L), f32),
            pltpu.VMEM((2, side, hr, dq), bf16),
            pltpu.VMEM((2, side, hr, dq), bf16),
            pltpu.VMEM((2, side, hr, dq), bf16),
            pltpu.VMEM((2, hr, dq), bf16),
            dma((rows // BLK + 1,)),
            dma((4, nc - 1)),
            dma((4, nc - 1)),
            dma((3, nd - 1)),
            dma((3, nd - 1)),
            dma((2, CHUNKS, side - 1)),
            dma((2, CHUNKS, side - 1)),
            dma((2, CHUNKS, side - 1)),
            dma((2, CHUNKS, side - 1)),
            dma((2, CHUNKS, side - 1)),
            dma((2, CHUNKS, side - 1)),
            dma((2, CHUNKS)),
        ],
        compiler_params=pltpu.CompilerParams(
            collective_id=0, has_side_effects=True, vmem_limit_bytes=56 * 2**20
        ),
        cost_estimate=pl.CostEstimate(
            flops=4 * rows * kc * d, bytes_accessed=2 * (rows + 2 * kc) * d, transcendentals=2 * rows * kc
        ),
        name="sinkhorn",
    )(col_start.reshape(nj, L), centroids, embeddings)
    parts = (out, row_potential, col_potential)
    out, row_potential, col_potential = pl.pallas_call(
        closing,
        out_shape=tuple(jax.ShapeDtypeStruct(part.shape, part.dtype) for part in parts),
        in_specs=[anywhere] * 3,
        out_specs=(anywhere,) * 3,
        scratch_shapes=[pltpu.VMEM(part.shape, part.dtype) for part in parts] + [dma((6,)), dma((6,))],
        name="closing",
    )(*parts)
    return out, row_potential.reshape(rows), col_potential.reshape(kc)


def solution(mesh):
    return jax.shard_map(
        functools.partial(on_device, mesh.shape["dp"], mesh.shape["cent"]),
        mesh=mesh,
        in_specs=(P("dp", None), P("cent", None), P("cent")),
        out_specs=(P("cent", None), P("dp"), P("cent")),
        check_vma=False,
    )
```

```python
import functools
import math

import jax
import jax.numpy as jnp
from jax import lax
from jax.experimental import pallas as pl
from jax.experimental.pallas import tpu as pltpu
from jax.sharding import PartitionSpec as P

MESH = pl.DeviceIdType.MESH
LOG2E = math.log2(math.e)
LN2 = math.log(2.0)
L = 128
BLK = 256
SUB = 128
SUB1 = 64
CHUNKS = 2


def diag_mask():
    return lax.broadcasted_iota(jnp.int32, (L, L), 0) == lax.broadcasted_iota(jnp.int32, (L, L), 1)


def to_column(row):
    spread = jnp.where(diag_mask(), jnp.broadcast_to(row, (L, L)), 0.0)
    return jnp.broadcast_to(jnp.sum(spread, axis=1, keepdims=True), (L, L))


def to_row(column):
    return jnp.sum(jnp.where(diag_mask(), column, 0.0), axis=0, keepdims=True)


def fold(x, act):
    while x.shape[0] > 8:
        half = x.shape[0] // 2
        x = act(x[:half], x[half:])
    return x


def kernel(
    nd, nc, side, n_total, k_total,
    g_ref, c_hbm, e_hbm,
    out_hbm, rp_ref, cp_ref,
    cv, ev, tm, am, bm, gcol, col1, col2, rrow, crow, rsum,
    l_all, rho2, rho3, lc_all, cs2, cs3,
    p1s, p1r, p2r, p3s,
    load_sem, rs_sem, rr_sem, cs_sem, cr_sem,
    b1s_sem, b1r_sem, b2s_sem, b2r_sem, b3s_sem, b3r_sem, own_sem,
):
    kc, d = cv.shape
    nk = tm.shape[0]
    nb = nk * L // BLK
    nj = kc // L
    dp = lax.axis_index("dp")
    ce = lax.axis_index("cent")
    x, y = dp // side, lax.rem(dp, side)

    cent_offsets = sorted(
        ((dz, dc) for dz in range(nc // 2) for dc in range(2) if dz or dc),
        key=lambda o: (-min(o[0], nc // 2 - o[0]), o),
    )
    dp_offsets = sorted(
        ((dx, dy) for dx in range(side) for dy in range(side) if dx or dy),
        key=lambda o: (-min(o[0], side - o[0]) - min(o[1], side - o[1]), o),
    )
    z, core = ce // 2, lax.rem(ce, 2)

    def cent_at(o, sign):
        return lax.rem(z + sign * o[0] + nc // 2, nc // 2) * 2 + lax.rem(core + o[1], 2)

    def dp_at(o, sign):
        return lax.rem(x + sign * o[0] + side, side) * side + lax.rem(y + sign * o[1] + side, side)

    c_load = pltpu.make_async_copy(c_hbm, cv, load_sem.at[nb])
    c_load.start()

    def e_load(b):
        rows = pl.ds(b * BLK, BLK)
        return pltpu.make_async_copy(e_hbm.at[rows], ev.at[rows], load_sem.at[b])

    for b in range(nb):
        e_load(b).start()

    barrier = pltpu.get_barrier_semaphore()
    for o in cent_offsets:
        pl.semaphore_signal(barrier, inc=1, device_id=(dp, cent_at(o, 1)), device_id_type=MESH)
    for o in dp_offsets:
        pl.semaphore_signal(barrier, inc=1, device_id=(dp_at(o, 1), ce), device_id_type=MESH)

    for t in range(nj):
        gcol[pl.ds(t * L, L), :] = to_column(g_ref[pl.ds(t, 1), :] * LOG2E)
    c_load.wait()

    scale = LOG2E / math.sqrt(d)

    def score_block(b, carry):
        e_load(b).wait()
        block = ev[pl.ds(pl.multiple_of(b * BLK, BLK), BLK), :]
        product = lax.dot_general(cv[...], block, (((1,), (1,)), ((), ())), preferred_element_type=jnp.float32)
        product = product * scale
        for h in range(BLK // L):
            tm[b * (BLK // L) + h] = product[:, h * L : (h + 1) * L]
        for h in range(BLK // L):
            k = b * (BLK // L) + h
            peak = jnp.max(fold(tm[k] + gcol[...], jnp.maximum), axis=0, keepdims=True)
            mass = jnp.sum(fold(jnp.exp2(tm[k] + gcol[...] - peak), jnp.add), axis=0, keepdims=True)
            l_all[ce, pl.ds(k, 1), :] = peak + jnp.log2(mass)
        return carry

    def cent_copy(phase, ref, k):
        return pltpu.make_async_remote_copy(
            src_ref=ref(ce), dst_ref=ref(ce),
            send_sem=rs_sem.at[phase, k], recv_sem=rr_sem.at[phase, k],
            device_id=(dp, cent_at(cent_offsets[k], 1)), device_id_type=MESH,
        )

    def cent_arrival(phase, ref, k):
        fr = cent_at(cent_offsets[k], -1)
        return pltpu.make_async_remote_copy(
            src_ref=ref(fr), dst_ref=ref(fr),
            send_sem=rs_sem.at[phase, k], recv_sem=rr_sem.at[phase, k],
            device_id=(dp, fr), device_id_type=MESH,
        )

    def dp_copy(phase, buf, k):
        return pltpu.make_async_remote_copy(
            src_ref=buf.at[dp], dst_ref=buf.at[dp],
            send_sem=cs_sem.at[phase, k], recv_sem=cr_sem.at[phase, k],
            device_id=(dp_at(dp_offsets[k], 1), ce), device_id_type=MESH,
        )

    def dp_arrival(phase, buf, k):
        fr = dp_at(dp_offsets[k], -1)
        return pltpu.make_async_remote_copy(
            src_ref=buf.at[fr], dst_ref=buf.at[fr],
            send_sem=cs_sem.at[phase, k], recv_sem=cr_sem.at[phase, k],
            device_id=(fr, ce), device_id_type=MESH,
        )

    def cent_start(phase, ref):
        for k in range(nc - 1):
            cent_copy(phase, ref, k).start()

    def cent_finish(phase, ref):
        for k in reversed(range(nc - 1)):
            cent_arrival(phase, ref, k).wait_recv()

    def dp_start(phase, buf):
        for k in range(nd - 1):
            dp_copy(phase, buf, k).start()

    def dp_finish(phase, buf):
        for k in reversed(range(nd - 1)):
            dp_arrival(phase, buf, k).wait_recv()

    early = nk // 2
    part_a = pl.ds(0, early)
    part_b = pl.ds(early, nk - early)

    def l_part(part):
        return lambda s: l_all.at[s, part]

    def whole_of(buf):
        return lambda s: buf.at[s]

    def joined(buf, n):
        peak = buf[0]
        for s in range(1, n):
            peak = jnp.maximum(peak, buf[s])
        total = jnp.exp2(buf[0] - peak)
        for s in range(1, n):
            total = total + jnp.exp2(buf[s] - peak)
        return peak + jnp.log2(total)

    def added(buf, n):
        total = buf[0].astype(jnp.float32)
        for s in range(1, n):
            total = total + buf[s].astype(jnp.float32)
        return total

    lax.fori_loop(0, early * L // BLK, score_block, 0)
    pl.semaphore_wait(barrier, nc - 1 + nd - 1)
    cent_start(0, l_part(part_a))
    lax.fori_loop(early * L // BLK, nb, score_block, 0)
    cent_start(1, l_part(part_b))
    cent_finish(0, l_part(part_a))
    cent_finish(1, l_part(part_b))

    rrow[...] = -math.log2(n_total) - joined(l_all, nc)

    def first_columns(jb, carry):
        rows = pl.ds(pl.multiple_of(jb * SUB1, SUB1), SUB1)
        peak = tm[0, rows, :] + rrow[pl.ds(0, 1), :]
        for k in range(1, nk):
            peak = jnp.maximum(peak, tm[k, rows, :] + rrow[pl.ds(k, 1), :])
        peak = jnp.broadcast_to(jnp.max(peak, axis=1, keepdims=True), (SUB1, L))
        mass = jnp.zeros((SUB1, L), jnp.float32)
        for k in range(nk):
            value = jnp.exp2(tm[k, rows, :] + rrow[pl.ds(k, 1), :] - peak)
            am[k, rows, :] = value
            mass = mass + value
        col1[rows, :] = peak
        col2[rows, :] = jnp.broadcast_to(jnp.sum(mass, axis=1, keepdims=True), (SUB1, L))
        return carry

    lax.fori_loop(0, kc // SUB1, first_columns, 0, unroll=2)
    for t in range(nj):
        top = to_row(col1[pl.ds(t * L, L), :])
        crow[pl.ds(t, 1), :] = top
        lc_all[dp, pl.ds(t, 1), :] = top + jnp.log2(to_row(col2[pl.ds(t * L, L), :]))
    dp_start(0, lc_all)
    dp_finish(0, lc_all)
    g_one = -math.log2(k_total) - joined(lc_all, nd)
    lift = jnp.exp2(crow[...] + g_one)
    crow[...] = g_one
    for t in range(nj):
        col1[pl.ds(t * L, L), :] = to_column(lift[t : t + 1, :])

    def second_rows(k, carry):
        value = am[k] * col1[...]
        am[k] = value
        rsum[pl.ds(k, 1), :] = jnp.sum(fold(value, jnp.add), axis=0, keepdims=True)
        return carry

    lax.fori_loop(0, nk, second_rows, 0, unroll=2)
    rho2[ce] = rsum[...].astype(rho2.dtype)
    cent_start(2, whole_of(rho2))
    cent_finish(2, whole_of(rho2))
    u_two = 1.0 / (n_total * added(rho2, nc))

    def column_sums(u, target, keep):
        def body(jb, carry):
            rows = pl.ds(pl.multiple_of(jb * SUB, SUB), SUB)
            mass = jnp.zeros((SUB, L), jnp.float32)
            for k in range(nk):
                value = am[k, rows, :] * u[k : k + 1, :]
                if keep:
                    bm[rows, k * L : (k + 1) * L] = value.astype(jnp.bfloat16)
                mass = mass + value
            col2[rows, :] = jnp.broadcast_to(jnp.sum(mass, axis=1, keepdims=True), (SUB, L))
            return carry

        lax.fori_loop(0, kc // SUB, body, 0, unroll=2)
        for t in range(nj):
            target[dp, pl.ds(t, 1), :] = to_row(col2[pl.ds(t * L, L), :])

    column_sums(u_two, cs2, False)
    dp_start(1, cs2)
    dp_finish(1, cs2)
    v_two = 1.0 / (k_total * added(cs2, nd))
    for t in range(nj):
        col1[pl.ds(t * L, L), :] = to_column(v_two[t : t + 1, :])

    def third_rows(k, carry):
        rho3[ce, pl.ds(k, 1), :] = jnp.sum(fold(am[k] * col1[...], jnp.add), axis=0, keepdims=True)
        return carry

    lax.fori_loop(0, nk, third_rows, 0, unroll=2)
    cent_start(3, whole_of(rho3))
    cent_finish(3, whole_of(rho3))
    u_three = 1.0 / (n_total * added(rho3, nc))
    rp_ref[...] = (rrow[...] + jnp.log2(u_three)) * LN2

    column_sums(u_three, cs3, True)
    dp_start(2, cs3)

    hr = kc // 2
    cr = hr // CHUNKS
    dq = d // side
    here = (x, y)
    offsets = sorted(range(1, side), key=lambda o: -min(o, side - o))

    def along(h, stage, i):
        if (h + stage) % 2 == 0:
            return (i * side + y, ce)
        return (x * side + i, ce)

    def place(h, stage, o=0):
        return lax.rem(here[(h + stage) % 2] + o + side, side)

    def chunk(c):
        return pl.ds(c * cr, cr)

    def b1(h, c, n, to, fr):
        return pltpu.make_async_remote_copy(
            src_ref=p1s.at[h, to, chunk(c)], dst_ref=p1r.at[h, fr, chunk(c)],
            send_sem=b1s_sem.at[h, c, n], recv_sem=b1r_sem.at[h, c, n],
            device_id=along(h, 0, to), device_id_type=MESH,
        )

    def b2(h, c, n, to, fr):
        return pltpu.make_async_remote_copy(
            src_ref=p2r.at[h, fr, chunk(c)], dst_ref=p2r.at[h, fr, chunk(c)],
            send_sem=b2s_sem.at[h, c, n], recv_sem=b2r_sem.at[h, c, n],
            device_id=along(h, 1, to), device_id_type=MESH,
        )

    def out_part(h, c, i):
        return out_hbm.at[pl.ds(h * hr + c * cr, cr), pl.ds(pl.multiple_of(i * dq, L), dq)]

    def b3(h, c, n, to, fr):
        return pltpu.make_async_remote_copy(
            src_ref=p3s.at[h, chunk(c)], dst_ref=out_part(h, c, fr),
            send_sem=b3s_sem.at[h, c, n], recv_sem=b3r_sem.at[h, c, n],
            device_id=along(h, 0, to), device_id_type=MESH,
        )

    def sending(copy, stage, h, c, n):
        return copy(h, c, n, place(h, stage, offsets[n]), place(h, stage))

    def arriving(copy, stage, h, c, n):
        return copy(h, c, n, place(h, stage), place(h, stage, -offsets[n]))

    def block_of(h, c, i):
        cols = pl.ds(pl.multiple_of(i * dq, L), dq)
        rows = pl.ds(h * hr + c * cr, cr)
        return jnp.dot(bm[rows, :], ev[:, cols], preferred_element_type=jnp.float32).astype(jnp.bfloat16)

    pieces = [(c, h) for c in range(CHUNKS) for h in range(2)]
    for c in range(CHUNKS):
        for n in range(side - 1):
            for h in range(2):
                p1s[h, place(h, 0, offsets[n]), chunk(c)] = block_of(h, c, place(h, 0, offsets[n]))
                sending(b1, 0, h, c, n).start()
        for h in range(2):
            p1r[h, place(h, 0), chunk(c)] = block_of(h, c, place(h, 0))

    def summed(buf, h, c):
        total = buf[h, 0, chunk(c)].astype(jnp.float32)
        for i in range(1, side):
            total = total + buf[h, i, chunk(c)].astype(jnp.float32)
        return total

    for c, h in pieces:
        for n in reversed(range(side - 1)):
            arriving(b1, 0, h, c, n).wait_recv()
        p2r[h, place(h, 1), chunk(c)] = summed(p1r, h, c).astype(jnp.bfloat16)
        for n in range(side - 1):
            sending(b2, 1, h, c, n).start()

    dp_finish(2, cs3)
    total = added(cs3, nd)
    cp_ref[...] = (crow[...] - jnp.log2(k_total * total)) * LN2
    back = 1.0 / total
    for t in range(nj):
        col1[pl.ds(t * L, L), :] = to_column(back[t : t + 1, :])

    own = []
    for c, h in pieces:
        for n in reversed(range(side - 1)):
            arriving(b2, 1, h, c, n).wait_recv()
        whole = summed(p2r, h, c)
        factor = col1[pl.ds(h * hr + c * cr, cr), :]
        for q in range(dq // L):
            p3s[h, chunk(c), q * L : (q + 1) * L] = (whole[:, q * L : (q + 1) * L] * factor).astype(jnp.bfloat16)
        for n in range(side - 1):
            sending(b3, 0, h, c, n).start()
        keep = pltpu.make_async_copy(p3s.at[h, chunk(c)], out_part(h, c, place(h, 0)), own_sem.at[h, c])
        keep.start()
        own.append(keep)

    for phase, ref in enumerate((l_part(part_a), l_part(part_b), whole_of(rho2), whole_of(rho3))):
        for k in range(nc - 1):
            cent_copy(phase, ref, k).wait_send()
    for phase, buf in enumerate((lc_all, cs2, cs3)):
        for k in range(nd - 1):
            dp_copy(phase, buf, k).wait_send()
    for c, h in pieces:
        for n in range(side - 1):
            sending(b1, 0, h, c, n).wait_send()
            sending(b2, 1, h, c, n).wait_send()
    for c, h in pieces:
        for n in reversed(range(side - 1)):
            arriving(b3, 0, h, c, n).wait_recv()
    for keep in own:
        keep.wait()
    for c, h in pieces:
        for n in range(side - 1):
            sending(b3, 0, h, c, n).wait_send()


def closing(c_in, r_in, k_in, c_out, r_out, k_out, c_v, r_v, k_v, in_sem, out_sem):
    step = c_v.shape[0] // 4
    parts = [(c_in.at[pl.ds(i * step, step)], c_v.at[pl.ds(i * step, step)], c_out.at[pl.ds(i * step, step)]) for i in range(4)]
    parts += [(r_in, r_v, r_out), (k_in, k_v, k_out)]
    arriving = [pltpu.make_async_copy(a, b, in_sem.at[i]) for i, (a, b, _) in enumerate(parts)]
    leaving = [pltpu.make_async_copy(b, c, out_sem.at[i]) for i, (_, b, c) in enumerate(parts)]
    for copy in arriving:
        copy.start()
    for a, b in zip(arriving, leaving):
        a.wait()
        b.start()
    for copy in leaving:
        copy.wait()


def on_device(nd, nc, embeddings, centroids, col_start):
    rows, d = embeddings.shape
    kc = centroids.shape[0]
    side = math.isqrt(nd)
    nk, nj = rows // L, kc // L
    hr, dq = kc // 2, d // side
    f32, bf16 = jnp.float32, jnp.bfloat16
    dma = pltpu.SemaphoreType.DMA
    vmem = pl.BlockSpec(memory_space=pltpu.VMEM)
    anywhere = pl.BlockSpec(memory_space=pl.ANY)
    out, row_potential, col_potential = pl.pallas_call(
        functools.partial(kernel, nd, nc, side, float(rows * nd), float(kc * nc)),
        out_shape=(
            jax.ShapeDtypeStruct((kc, d), bf16),
            jax.ShapeDtypeStruct((nk, L), f32),
            jax.ShapeDtypeStruct((nj, L), f32),
        ),
        in_specs=[vmem, anywhere, anywhere],
        out_specs=(anywhere, vmem, vmem),
        scratch_shapes=[
            pltpu.VMEM((kc, d), bf16),
            pltpu.VMEM((rows, d), bf16),
            pltpu.VMEM((nk, kc, L), f32),
            pltpu.VMEM((nk, kc, L), f32),
            pltpu.VMEM((kc, rows), bf16),
            pltpu.VMEM((kc, L), f32),
            pltpu.VMEM((kc, L), f32),
            pltpu.VMEM((kc, L), f32),
            pltpu.VMEM((nk, L), f32),
            pltpu.VMEM((nj, L), f32),
            pltpu.VMEM((nk, L), f32),
            pltpu.VMEM((nc, nk, L), f32),
            pltpu.VMEM((nc, nk, L), bf16),
            pltpu.VMEM((nc, nk, L), f32),
            pltpu.VMEM((nd, nj, L), f32),
            pltpu.VMEM((nd, nj, L), f32),
            pltpu.VMEM((nd, nj, L), f32),
            pltpu.VMEM((2, side, hr, dq), bf16),
            pltpu.VMEM((2, side, hr, dq), bf16),
            pltpu.VMEM((2, side, hr, dq), bf16),
            pltpu.VMEM((2, hr, dq), bf16),
            dma((rows // BLK + 1,)),
            dma((4, nc - 1)),
            dma((4, nc - 1)),
            dma((3, nd - 1)),
            dma((3, nd - 1)),
            dma((2, CHUNKS, side - 1)),
            dma((2, CHUNKS, side - 1)),
            dma((2, CHUNKS, side - 1)),
            dma((2, CHUNKS, side - 1)),
            dma((2, CHUNKS, side - 1)),
            dma((2, CHUNKS, side - 1)),
            dma((2, CHUNKS)),
        ],
        compiler_params=pltpu.CompilerParams(
            collective_id=0, has_side_effects=True, vmem_limit_bytes=56 * 2**20
        ),
        cost_estimate=pl.CostEstimate(
            flops=4 * rows * kc * d, bytes_accessed=2 * (rows + 2 * kc) * d, transcendentals=2 * rows * kc
        ),
        name="sinkhorn",
    )(col_start.reshape(nj, L), centroids, embeddings)
    parts = (out, row_potential, col_potential)
    out, row_potential, col_potential = pl.pallas_call(
        closing,
        out_shape=tuple(jax.ShapeDtypeStruct(part.shape, part.dtype) for part in parts),
        in_specs=[anywhere] * 3,
        out_specs=(anywhere,) * 3,
        scratch_shapes=[pltpu.VMEM(part.shape, part.dtype) for part in parts] + [dma((6,)), dma((6,))],
        name="closing",
    )(*parts)
    return out, row_potential.reshape(rows), col_potential.reshape(kc)


def solution(mesh):
    return jax.shard_map(
        functools.partial(on_device, mesh.shape["dp"], mesh.shape["cent"]),
        mesh=mesh,
        in_specs=(P("dp", None), P("cent", None), P("cent")),
        out_specs=(P("cent", None), P("dp"), P("cent")),
        check_vma=False,
    )
```

```python
import functools
import math

import jax
import jax.numpy as jnp
from jax import lax
from jax.experimental import pallas as pl
from jax.experimental.pallas import tpu as pltpu
from jax.sharding import PartitionSpec as P

MESH = pl.DeviceIdType.MESH
LOG2E = math.log2(math.e)
LN2 = math.log(2.0)
L = 128
BLK = 256
SUB = 128
SUB1 = 64
CHUNKS = 2
MATS = 2
PIECES = 4


def diag_mask():
    return lax.broadcasted_iota(jnp.int32, (L, L), 0) == lax.broadcasted_iota(jnp.int32, (L, L), 1)


def to_column(row):
    spread = jnp.where(diag_mask(), jnp.broadcast_to(row, (L, L)), 0.0)
    return jnp.broadcast_to(jnp.sum(spread, axis=1, keepdims=True), (L, L))


def to_row(column):
    return jnp.sum(jnp.where(diag_mask(), column, 0.0), axis=0, keepdims=True)


def fold(x, act):
    while x.shape[0] > 8:
        half = x.shape[0] // 2
        x = act(x[:half], x[half:])
    return x


def kernel(
    nd, nc, side, n_total, k_total,
    g_hbm, c_hbm, e_hbm,
    out_hbm, rp_ref, cp_ref,
    g_ref, cv, ev, tm, am, bm, gcol, col1, col2, rrow, crow, rsum,
    l_all, rho2, rho3, lc_all, cs2, cs3,
    p1s, p1r, p2r, p3s,
    load_sem, rs_sem, rr_sem, cs_sem, cr_sem,
    b1s_sem, b1r_sem, b2s_sem, b2r_sem, b3s_sem, b3r_sem, own_sem,
):
    kc, d = cv.shape
    nk = tm.shape[0]
    nb = nk * L // BLK
    nj = kc // L
    dp = lax.axis_index("dp")
    ce = lax.axis_index("cent")
    x, y = dp // side, lax.rem(dp, side)

    cent_offsets = sorted(
        ((dz, dc) for dz in range(nc // 2) for dc in range(2) if dz or dc),
        key=lambda o: (-min(o[0], nc // 2 - o[0]), o),
    )
    dp_offsets = sorted(
        ((dx, dy) for dx in range(side) for dy in range(side) if dx or dy),
        key=lambda o: (-min(o[0], side - o[0]) - min(o[1], side - o[1]), o),
    )
    z, core = ce // 2, lax.rem(ce, 2)

    def cent_at(o, sign):
        return lax.rem(z + sign * o[0] + nc // 2, nc // 2) * 2 + lax.rem(core + o[1], 2)

    def dp_at(o, sign):
        return lax.rem(x + sign * o[0] + side, side) * side + lax.rem(y + sign * o[1] + side, side)

    c_load = pltpu.make_async_copy(c_hbm, cv, load_sem.at[nb])
    g_load = pltpu.make_async_copy(g_hbm, g_ref, load_sem.at[nb + 1])
    c_load.start()
    g_load.start()

    def e_load(b):
        rows = pl.ds(b * BLK, BLK)
        return pltpu.make_async_copy(e_hbm.at[rows], ev.at[rows], load_sem.at[b])

    for b in range(nb):
        e_load(b).start()

    barrier = pltpu.get_barrier_semaphore()
    for o in cent_offsets:
        pl.semaphore_signal(barrier, inc=1, device_id=(dp, cent_at(o, 1)), device_id_type=MESH)
    for o in dp_offsets:
        pl.semaphore_signal(barrier, inc=1, device_id=(dp_at(o, 1), ce), device_id_type=MESH)

    g_load.wait()
    for t in range(nj):
        gcol[pl.ds(t * L, L), :] = to_column(g_ref[pl.ds(t, 1), :] * LOG2E)
    c_load.wait()

    scale = LOG2E / math.sqrt(d)

    def score_block(b, carry):
        e_load(b).wait()
        block = ev[pl.ds(pl.multiple_of(b * BLK, BLK), BLK), :]
        product = lax.dot_general(cv[...], block, (((1,), (1,)), ((), ())), preferred_element_type=jnp.float32)
        product = product * scale
        for h in range(BLK // L):
            tm[b * (BLK // L) + h] = product[:, h * L : (h + 1) * L]
        for h in range(BLK // L):
            k = b * (BLK // L) + h
            peak = jnp.max(fold(tm[k] + gcol[...], jnp.maximum), axis=0, keepdims=True)
            mass = jnp.sum(fold(jnp.exp2(tm[k] + gcol[...] - peak), jnp.add), axis=0, keepdims=True)
            l_all[ce, pl.ds(k, 1), :] = peak + jnp.log2(mass)
        return carry

    def cent_copy(phase, ref, k):
        return pltpu.make_async_remote_copy(
            src_ref=ref(ce), dst_ref=ref(ce),
            send_sem=rs_sem.at[phase, k], recv_sem=rr_sem.at[phase, k],
            device_id=(dp, cent_at(cent_offsets[k], 1)), device_id_type=MESH,
        )

    def cent_arrival(phase, ref, k):
        fr = cent_at(cent_offsets[k], -1)
        return pltpu.make_async_remote_copy(
            src_ref=ref(fr), dst_ref=ref(fr),
            send_sem=rs_sem.at[phase, k], recv_sem=rr_sem.at[phase, k],
            device_id=(dp, fr), device_id_type=MESH,
        )

    def dp_copy(phase, buf, k):
        return pltpu.make_async_remote_copy(
            src_ref=buf.at[dp], dst_ref=buf.at[dp],
            send_sem=cs_sem.at[phase, k], recv_sem=cr_sem.at[phase, k],
            device_id=(dp_at(dp_offsets[k], 1), ce), device_id_type=MESH,
        )

    def dp_arrival(phase, buf, k):
        fr = dp_at(dp_offsets[k], -1)
        return pltpu.make_async_remote_copy(
            src_ref=buf.at[fr], dst_ref=buf.at[fr],
            send_sem=cs_sem.at[phase, k], recv_sem=cr_sem.at[phase, k],
            device_id=(fr, ce), device_id_type=MESH,
        )

    def cent_start(phase, ref):
        for k in range(nc - 1):
            cent_copy(phase, ref, k).start()

    def cent_finish(phase, ref):
        for k in reversed(range(nc - 1)):
            cent_arrival(phase, ref, k).wait_recv()

    def dp_start(phase, buf):
        for k in range(nd - 1):
            dp_copy(phase, buf, k).start()

    def dp_finish(phase, buf):
        for k in reversed(range(nd - 1)):
            dp_arrival(phase, buf, k).wait_recv()

    early = nk // 2
    part_a = pl.ds(0, early)
    part_b = pl.ds(early, nk - early)

    def l_part(part):
        return lambda s: l_all.at[s, part]

    def whole_of(buf):
        return lambda s: buf.at[s]

    def joined(buf, n):
        peak = buf[0]
        for s in range(1, n):
            peak = jnp.maximum(peak, buf[s])
        total = jnp.exp2(buf[0] - peak)
        for s in range(1, n):
            total = total + jnp.exp2(buf[s] - peak)
        return peak + jnp.log2(total)

    def added(buf, n):
        total = buf[0].astype(jnp.float32)
        for s in range(1, n):
            total = total + buf[s].astype(jnp.float32)
        return total

    lax.fori_loop(0, early * L // BLK, score_block, 0)
    pl.semaphore_wait(barrier, nc - 1 + nd - 1)
    cent_start(0, l_part(part_a))
    lax.fori_loop(early * L // BLK, nb, score_block, 0)
    cent_start(1, l_part(part_b))
    cent_finish(0, l_part(part_a))
    cent_finish(1, l_part(part_b))

    rrow[...] = -math.log2(n_total) - joined(l_all, nc)

    def first_columns(jb, carry):
        rows = pl.ds(pl.multiple_of(jb * SUB1, SUB1), SUB1)
        peak = tm[0, rows, :] + rrow[pl.ds(0, 1), :]
        for k in range(1, nk):
            peak = jnp.maximum(peak, tm[k, rows, :] + rrow[pl.ds(k, 1), :])
        peak = jnp.broadcast_to(jnp.max(peak, axis=1, keepdims=True), (SUB1, L))
        mass = jnp.zeros((SUB1, L), jnp.float32)
        for k in range(nk):
            value = jnp.exp2(tm[k, rows, :] + rrow[pl.ds(k, 1), :] - peak)
            am[k, rows, :] = value
            mass = mass + value
        col1[rows, :] = peak
        col2[rows, :] = jnp.broadcast_to(jnp.sum(mass, axis=1, keepdims=True), (SUB1, L))
        return carry

    lax.fori_loop(0, kc // SUB1, first_columns, 0, unroll=2)
    for t in range(nj):
        top = to_row(col1[pl.ds(t * L, L), :])
        crow[pl.ds(t, 1), :] = top
        lc_all[dp, pl.ds(t, 1), :] = top + jnp.log2(to_row(col2[pl.ds(t * L, L), :]))
    dp_start(0, lc_all)
    dp_finish(0, lc_all)
    g_one = -math.log2(k_total) - joined(lc_all, nd)
    lift = jnp.exp2(crow[...] + g_one)
    crow[...] = g_one
    for t in range(nj):
        col1[pl.ds(t * L, L), :] = to_column(lift[t : t + 1, :])

    def second_rows(k, carry):
        value = am[k] * col1[...]
        am[k] = value
        rsum[pl.ds(k, 1), :] = jnp.sum(fold(value, jnp.add), axis=0, keepdims=True)
        return carry

    lax.fori_loop(0, nk, second_rows, 0, unroll=2)
    rho2[ce] = rsum[...].astype(rho2.dtype)
    cent_start(2, whole_of(rho2))
    cent_finish(2, whole_of(rho2))
    u_two = 1.0 / (n_total * added(rho2, nc))

    def column_block(u, start, size, keep):
        rows = pl.ds(start, size)
        mass = jnp.zeros((size, L), jnp.float32)
        for k in range(nk):
            value = am[k, rows, :] * u[k : k + 1, :]
            if keep:
                bm[rows, k * L : (k + 1) * L] = value.astype(jnp.bfloat16)
            mass = mass + value
        col2[rows, :] = jnp.broadcast_to(jnp.sum(mass, axis=1, keepdims=True), (size, L))

    def column_rows(target):
        for t in range(nj):
            target[dp, pl.ds(t, 1), :] = to_row(col2[pl.ds(t * L, L), :])

    for start in range(0, kc, SUB):
        column_block(u_two, start, SUB, False)
    column_rows(cs2)
    dp_start(1, cs2)
    dp_finish(1, cs2)
    v_two = 1.0 / (k_total * added(cs2, nd))
    for t in range(nj):
        col1[pl.ds(t * L, L), :] = to_column(v_two[t : t + 1, :])

    def third_rows(k, carry):
        rho3[ce, pl.ds(k, 1), :] = jnp.sum(fold(am[k] * col1[...], jnp.add), axis=0, keepdims=True)
        return carry

    lax.fori_loop(0, nk, third_rows, 0, unroll=2)
    cent_start(3, whole_of(rho3))
    cent_finish(3, whole_of(rho3))
    u_three = 1.0 / (n_total * added(rho3, nc))
    rp_ref[...] = (rrow[...] + jnp.log2(u_three)) * LN2


    hr = kc // 2
    cr = hr // CHUNKS
    dq = d // side
    here = (x, y)
    offsets = sorted(range(1, side), key=lambda o: -min(o, side - o))

    def along(h, stage, i):
        if (h + stage) % 2 == 0:
            return (i * side + y, ce)
        return (x * side + i, ce)

    def place(h, stage, o=0):
        return lax.rem(here[(h + stage) % 2] + o + side, side)

    def chunk(c):
        return pl.ds(c * cr, cr)

    def b1(h, c, n, to, fr):
        return pltpu.make_async_remote_copy(
            src_ref=p1s.at[h, to, chunk(c)], dst_ref=p1r.at[h, fr, chunk(c)],
            send_sem=b1s_sem.at[h, c, n], recv_sem=b1r_sem.at[h, c, n],
            device_id=along(h, 0, to), device_id_type=MESH,
        )

    def b2(h, c, n, to, fr):
        return pltpu.make_async_remote_copy(
            src_ref=p2r.at[h, fr, chunk(c)], dst_ref=p2r.at[h, fr, chunk(c)],
            send_sem=b2s_sem.at[h, c, n], recv_sem=b2r_sem.at[h, c, n],
            device_id=along(h, 1, to), device_id_type=MESH,
        )

    def out_part(h, c, i):
        return out_hbm.at[pl.ds(h * hr + c * cr, cr), pl.ds(pl.multiple_of(i * dq, L), dq)]

    def b3(h, c, n, to, fr):
        return pltpu.make_async_remote_copy(
            src_ref=p3s.at[h, chunk(c)], dst_ref=out_part(h, c, fr),
            send_sem=b3s_sem.at[h, c, n], recv_sem=b3r_sem.at[h, c, n],
            device_id=along(h, 0, to), device_id_type=MESH,
        )

    def sending(copy, stage, h, c, n):
        return copy(h, c, n, place(h, stage, offsets[n]), place(h, stage))

    def arriving(copy, stage, h, c, n):
        return copy(h, c, n, place(h, stage), place(h, stage, -offsets[n]))

    pieces = [(c, h) for c in range(CHUNKS) for h in range(2)]
    per = CHUNKS // MATS
    mr = hr // MATS

    def product_step(m, n, o):
        for h in range(2):
            i = place(h, 0, o)
            cols = pl.ds(pl.multiple_of(i * dq, L), dq)
            rows = pl.ds(m * mr, mr)
            block = jnp.dot(bm[pl.ds(h * hr + m * mr, mr), :], ev[:, cols], preferred_element_type=jnp.float32)
            block = block.astype(jnp.bfloat16)
            if n is None:
                p1r[h, i, rows] = block
            else:
                p1s[h, i, rows] = block
                for c in range(m * per, (m + 1) * per):
                    b1(h, c, n, i, place(h, 0)).start()

    for m in range(MATS):
        for h in range(2):
            for start in range(h * hr + m * mr, h * hr + (m + 1) * mr, min(SUB, mr)):
                column_block(u_three, start, min(SUB, mr), True)
        if m == MATS - 1:
            column_rows(cs3)
            dp_start(2, cs3)
        for n in range(side - 1):
            product_step(m, n, offsets[n])
        product_step(m, None, 0)

    def summed(buf, h, c):
        total = buf[h, 0, chunk(c)].astype(jnp.float32)
        for i in range(1, side):
            total = total + buf[h, i, chunk(c)].astype(jnp.float32)
        return total

    for c, h in pieces:
        for n in reversed(range(side - 1)):
            arriving(b1, 0, h, c, n).wait_recv()
        p2r[h, place(h, 1), chunk(c)] = summed(p1r, h, c).astype(jnp.bfloat16)
        for n in range(side - 1):
            sending(b2, 1, h, c, n).start()

    dp_finish(2, cs3)
    total = added(cs3, nd)
    cp_ref[...] = (crow[...] - jnp.log2(k_total * total)) * LN2
    back = 1.0 / total
    for t in range(nj):
        col1[pl.ds(t * L, L), :] = to_column(back[t : t + 1, :])

    own = []
    for c, h in pieces:
        for n in reversed(range(side - 1)):
            arriving(b2, 1, h, c, n).wait_recv()
        whole = summed(p2r, h, c)
        factor = col1[pl.ds(h * hr + c * cr, cr), :]
        for q in range(dq // L):
            p3s[h, chunk(c), q * L : (q + 1) * L] = (whole[:, q * L : (q + 1) * L] * factor).astype(jnp.bfloat16)
        for n in range(side - 1):
            sending(b3, 0, h, c, n).start()
        keep = pltpu.make_async_copy(p3s.at[h, chunk(c)], out_part(h, c, place(h, 0)), own_sem.at[h, c])
        keep.start()
        own.append(keep)

    for phase, ref in enumerate((l_part(part_a), l_part(part_b), whole_of(rho2), whole_of(rho3))):
        for k in range(nc - 1):
            cent_copy(phase, ref, k).wait_send()
    for phase, buf in enumerate((lc_all, cs2, cs3)):
        for k in range(nd - 1):
            dp_copy(phase, buf, k).wait_send()
    for c, h in pieces:
        for n in range(side - 1):
            sending(b1, 0, h, c, n).wait_send()
            sending(b2, 1, h, c, n).wait_send()
    for c, h in pieces:
        for n in reversed(range(side - 1)):
            arriving(b3, 0, h, c, n).wait_recv()
    for keep in own:
        keep.wait()
    for c, h in pieces:
        for n in range(side - 1):
            sending(b3, 0, h, c, n).wait_send()


def closing(c_in, r_in, k_in, c_out, r_out, k_out, sem):
    step = c_in.shape[0] // PIECES
    pairs = [(c_in.at[pl.ds(i * step, step)], c_out.at[pl.ds(i * step, step)]) for i in range(PIECES)]
    pairs += [(r_in, r_out), (k_in, k_out)]
    copies = [pltpu.make_async_copy(a, b, sem.at[i]) for i, (a, b) in enumerate(pairs)]
    for copy in copies:
        copy.start()
    for copy in copies:
        copy.wait()


def on_device(nd, nc, embeddings, centroids, col_start):
    rows, d = embeddings.shape
    kc = centroids.shape[0]
    side = math.isqrt(nd)
    nk, nj = rows // L, kc // L
    hr, dq = kc // 2, d // side
    f32, bf16 = jnp.float32, jnp.bfloat16
    dma = pltpu.SemaphoreType.DMA
    vmem = pl.BlockSpec(memory_space=pltpu.VMEM)
    anywhere = pl.BlockSpec(memory_space=pl.ANY)
    out, row_potential, col_potential = pl.pallas_call(
        functools.partial(kernel, nd, nc, side, float(rows * nd), float(kc * nc)),
        out_shape=(
            pltpu.VMEM((kc, d), bf16),
            pltpu.VMEM((nk, L), f32),
            pltpu.VMEM((nj, L), f32),
        ),
        in_specs=[anywhere] * 3,
        out_specs=(vmem, vmem, vmem),
        scratch_shapes=[
            pltpu.VMEM((nj, L), f32),
            pltpu.VMEM((kc, d), bf16),
            pltpu.VMEM((rows, d), bf16),
            pltpu.VMEM((nk, kc, L), f32),
            pltpu.VMEM((nk, kc, L), f32),
            pltpu.VMEM((kc, rows), bf16),
            pltpu.VMEM((kc, L), f32),
            pltpu.VMEM((kc, L), f32),
            pltpu.VMEM((kc, L), f32),
            pltpu.VMEM((nk, L), f32),
            pltpu.VMEM((nj, L), f32),
            pltpu.VMEM((nk, L), f32),
            pltpu.VMEM((nc, nk, L), f32),
            pltpu.VMEM((nc, nk, L), bf16),
            pltpu.VMEM((nc, nk, L), f32),
            pltpu.VMEM((nd, nj, L), f32),
            pltpu.VMEM((nd, nj, L), f32),
            pltpu.VMEM((nd, nj, L), f32),
            pltpu.VMEM((2, side, hr, dq), bf16),
            pltpu.VMEM((2, side, hr, dq), bf16),
            pltpu.VMEM((2, side, hr, dq), bf16),
            pltpu.VMEM((2, hr, dq), bf16),
            dma((rows // BLK + 2,)),
            dma((4, nc - 1)),
            dma((4, nc - 1)),
            dma((3, nd - 1)),
            dma((3, nd - 1)),
            dma((2, CHUNKS, side - 1)),
            dma((2, CHUNKS, side - 1)),
            dma((2, CHUNKS, side - 1)),
            dma((2, CHUNKS, side - 1)),
            dma((2, CHUNKS, side - 1)),
            dma((2, CHUNKS, side - 1)),
            dma((2, CHUNKS)),
        ],
        compiler_params=pltpu.CompilerParams(
            collective_id=0, has_side_effects=True, vmem_limit_bytes=125 * 2**19
        ),
        cost_estimate=pl.CostEstimate(
            flops=4 * rows * kc * d, bytes_accessed=2 * (rows + 2 * kc) * d, transcendentals=2 * rows * kc
        ),
        name="sinkhorn",
    )(col_start.reshape(nj, L), centroids, embeddings)
    parts = (out, row_potential, col_potential)
    out, row_potential, col_potential = pl.pallas_call(
        closing,
        out_shape=tuple(jax.ShapeDtypeStruct(part.shape, part.dtype) for part in parts),
        in_specs=[vmem] * 3,
        out_specs=(anywhere,) * 3,
        scratch_shapes=[dma((PIECES + 2,))],
        name="closing",
    )(*(pltpu.with_memory_space_constraint(part, pltpu.VMEM) for part in parts))
    return out, row_potential.reshape(rows), col_potential.reshape(kc)


def solution(mesh):
    return jax.shard_map(
        functools.partial(on_device, mesh.shape["dp"], mesh.shape["cent"]),
        mesh=mesh,
        in_specs=(P("dp", None), P("cent", None), P("cent")),
        out_specs=(P("cent", None), P("dp"), P("cent")),
        check_vma=False,
    )
```

```python
import functools
import math

import jax
import jax.numpy as jnp
from jax import lax
from jax.experimental import pallas as pl
from jax.experimental.pallas import tpu as pltpu
from jax.sharding import PartitionSpec as P

MESH = pl.DeviceIdType.MESH
LOG2E = math.log2(math.e)
LN2 = math.log(2.0)
L = 128
BLK = 256
SUB = 128
SUB1 = 64
CHUNKS = 2
MATS = 2
PIECES = 4


def diag_mask():
    return lax.broadcasted_iota(jnp.int32, (L, L), 0) == lax.broadcasted_iota(jnp.int32, (L, L), 1)


def to_column(row):
    spread = jnp.where(diag_mask(), jnp.broadcast_to(row, (L, L)), 0.0)
    return jnp.broadcast_to(jnp.sum(spread, axis=1, keepdims=True), (L, L))


def to_row(column):
    return jnp.sum(jnp.where(diag_mask(), column, 0.0), axis=0, keepdims=True)


def fold(x, act):
    while x.shape[0] > 8:
        half = x.shape[0] // 2
        x = act(x[:half], x[half:])
    return x


def kernel(
    nd, nc, side, n_total, k_total,
    g_hbm, c_hbm, e_hbm,
    out_hbm, rp_ref, cp_ref,
    g_ref, cv, ev, tm, am, bm, gcol, col1, col2, rrow, crow, rsum,
    l_all, rho2, rho3, lc_all, cs2, cs3,
    p1s, p1r, p2r, p3s,
    load_sem, rs_sem, rr_sem, cs_sem, cr_sem,
    b1s_sem, b1r_sem, b2s_sem, b2r_sem, b3s_sem, b3r_sem, own_sem,
):
    kc, d = cv.shape
    nk = tm.shape[0]
    nb = nk * L // BLK
    nj = kc // L
    dp = lax.axis_index("dp")
    ce = lax.axis_index("cent")
    x, y = dp // side, lax.rem(dp, side)

    cent_offsets = sorted(
        ((dz, dc) for dz in range(nc // 2) for dc in range(2) if dz or dc),
        key=lambda o: (-min(o[0], nc // 2 - o[0]), o),
    )
    dp_offsets = sorted(
        ((dx, dy) for dx in range(side) for dy in range(side) if dx or dy),
        key=lambda o: (-min(o[0], side - o[0]) - min(o[1], side - o[1]), o),
    )
    z, core = ce // 2, lax.rem(ce, 2)

    def cent_at(o, sign):
        return lax.rem(z + sign * o[0] + nc // 2, nc // 2) * 2 + lax.rem(core + o[1], 2)

    def dp_at(o, sign):
        return lax.rem(x + sign * o[0] + side, side) * side + lax.rem(y + sign * o[1] + side, side)

    c_load = pltpu.make_async_copy(c_hbm, cv, load_sem.at[nb])
    g_load = pltpu.make_async_copy(g_hbm, g_ref, load_sem.at[nb + 1])
    c_load.start()
    g_load.start()

    def e_load(b):
        rows = pl.ds(b * BLK, BLK)
        return pltpu.make_async_copy(e_hbm.at[rows], ev.at[rows], load_sem.at[b])

    for b in range(nb):
        e_load(b).start()

    barrier = pltpu.get_barrier_semaphore()
    for o in cent_offsets:
        pl.semaphore_signal(barrier, inc=1, device_id=(dp, cent_at(o, 1)), device_id_type=MESH)
    for o in dp_offsets:
        pl.semaphore_signal(barrier, inc=1, device_id=(dp_at(o, 1), ce), device_id_type=MESH)

    g_load.wait()
    for t in range(nj):
        gcol[pl.ds(t * L, L), :] = to_column(g_ref[pl.ds(t, 1), :] * LOG2E)
    c_load.wait()

    scale = LOG2E / math.sqrt(d)

    def score_block(b, carry):
        e_load(b).wait()
        block = ev[pl.ds(pl.multiple_of(b * BLK, BLK), BLK), :]
        product = lax.dot_general(cv[...], block, (((1,), (1,)), ((), ())), preferred_element_type=jnp.float32)
        product = product * scale
        for h in range(BLK // L):
            tm[b * (BLK // L) + h] = product[:, h * L : (h + 1) * L]
        for h in range(BLK // L):
            k = b * (BLK // L) + h
            peak = jnp.max(fold(tm[k] + gcol[...], jnp.maximum), axis=0, keepdims=True)
            mass = jnp.sum(fold(jnp.exp2(tm[k] + gcol[...] - peak), jnp.add), axis=0, keepdims=True)
            l_all[ce, pl.ds(k, 1), :] = peak + jnp.log2(mass)
        return carry

    def cent_copy(phase, ref, k):
        return pltpu.make_async_remote_copy(
            src_ref=ref(ce), dst_ref=ref(ce),
            send_sem=rs_sem.at[phase, k], recv_sem=rr_sem.at[phase, k],
            device_id=(dp, cent_at(cent_offsets[k], 1)), device_id_type=MESH,
        )

    def cent_arrival(phase, ref, k):
        fr = cent_at(cent_offsets[k], -1)
        return pltpu.make_async_remote_copy(
            src_ref=ref(fr), dst_ref=ref(fr),
            send_sem=rs_sem.at[phase, k], recv_sem=rr_sem.at[phase, k],
            device_id=(dp, fr), device_id_type=MESH,
        )

    def dp_copy(phase, buf, k):
        return pltpu.make_async_remote_copy(
            src_ref=buf.at[dp], dst_ref=buf.at[dp],
            send_sem=cs_sem.at[phase, k], recv_sem=cr_sem.at[phase, k],
            device_id=(dp_at(dp_offsets[k], 1), ce), device_id_type=MESH,
        )

    def dp_arrival(phase, buf, k):
        fr = dp_at(dp_offsets[k], -1)
        return pltpu.make_async_remote_copy(
            src_ref=buf.at[fr], dst_ref=buf.at[fr],
            send_sem=cs_sem.at[phase, k], recv_sem=cr_sem.at[phase, k],
            device_id=(fr, ce), device_id_type=MESH,
        )

    def cent_start(phase, ref):
        for k in range(nc - 1):
            cent_copy(phase, ref, k).start()

    def cent_finish(phase, ref):
        for k in reversed(range(nc - 1)):
            cent_arrival(phase, ref, k).wait_recv()

    def dp_start(phase, buf):
        for k in range(nd - 1):
            dp_copy(phase, buf, k).start()

    def dp_finish(phase, buf):
        for k in reversed(range(nd - 1)):
            dp_arrival(phase, buf, k).wait_recv()

    early = nk // 2
    part_a = pl.ds(0, early)
    part_b = pl.ds(early, nk - early)

    def l_part(part):
        return lambda s: l_all.at[s, part]

    def whole_of(buf):
        return lambda s: buf.at[s]

    def joined(buf, n):
        peak = buf[0]
        for s in range(1, n):
            peak = jnp.maximum(peak, buf[s])
        total = jnp.exp2(buf[0] - peak)
        for s in range(1, n):
            total = total + jnp.exp2(buf[s] - peak)
        return peak + jnp.log2(total)

    def added(buf, n):
        total = buf[0].astype(jnp.float32)
        for s in range(1, n):
            total = total + buf[s].astype(jnp.float32)
        return total

    lax.fori_loop(0, early * L // BLK, score_block, 0)
    pl.semaphore_wait(barrier, nc - 1 + nd - 1)
    cent_start(0, l_part(part_a))
    lax.fori_loop(early * L // BLK, nb, score_block, 0)
    cent_start(1, l_part(part_b))
    cent_finish(0, l_part(part_a))
    cent_finish(1, l_part(part_b))

    rrow[...] = -math.log2(n_total) - joined(l_all, nc)

    def first_columns(jb, carry):
        rows = pl.ds(pl.multiple_of(jb * SUB1, SUB1), SUB1)
        peak = tm[0, rows, :] + rrow[pl.ds(0, 1), :]
        for k in range(1, nk):
            peak = jnp.maximum(peak, tm[k, rows, :] + rrow[pl.ds(k, 1), :])
        peak = jnp.broadcast_to(jnp.max(peak, axis=1, keepdims=True), (SUB1, L))
        mass = jnp.zeros((SUB1, L), jnp.float32)
        for k in range(nk):
            value = jnp.exp2(tm[k, rows, :] + rrow[pl.ds(k, 1), :] - peak)
            am[k, rows, :] = value
            mass = mass + value
        col1[rows, :] = peak
        col2[rows, :] = jnp.broadcast_to(jnp.sum(mass, axis=1, keepdims=True), (SUB1, L))
        return carry

    lax.fori_loop(0, kc // SUB1, first_columns, 0, unroll=2)
    for t in range(nj):
        top = to_row(col1[pl.ds(t * L, L), :])
        crow[pl.ds(t, 1), :] = top
        lc_all[dp, pl.ds(t, 1), :] = top + jnp.log2(to_row(col2[pl.ds(t * L, L), :]))
    dp_start(0, lc_all)
    dp_finish(0, lc_all)
    g_one = -math.log2(k_total) - joined(lc_all, nd)
    lift = jnp.exp2(crow[...] + g_one)
    crow[...] = g_one
    for t in range(nj):
        col1[pl.ds(t * L, L), :] = to_column(lift[t : t + 1, :])

    def second_rows(k, carry):
        value = am[k] * col1[...]
        am[k] = value
        rsum[pl.ds(k, 1), :] = jnp.sum(fold(value, jnp.add), axis=0, keepdims=True)
        return carry

    lax.fori_loop(0, nk, second_rows, 0, unroll=2)
    rho2[ce] = rsum[...].astype(rho2.dtype)
    cent_start(2, whole_of(rho2))
    cent_finish(2, whole_of(rho2))
    u_two = 1.0 / (n_total * added(rho2, nc))

    def column_block(u, start, size, keep):
        rows = pl.ds(start, size)
        mass = jnp.zeros((size, L), jnp.float32)
        for k in range(nk):
            value = am[k, rows, :] * u[k : k + 1, :]
            if keep:
                bm[rows, k * L : (k + 1) * L] = value.astype(jnp.bfloat16)
            mass = mass + value
        col2[rows, :] = jnp.broadcast_to(jnp.sum(mass, axis=1, keepdims=True), (size, L))

    def column_rows(target):
        for t in range(nj):
            target[dp, pl.ds(t, 1), :] = to_row(col2[pl.ds(t * L, L), :])

    for start in range(0, kc, SUB):
        column_block(u_two, start, SUB, False)
    column_rows(cs2)
    dp_start(1, cs2)
    dp_finish(1, cs2)
    v_two = 1.0 / (k_total * added(cs2, nd))
    for t in range(nj):
        col1[pl.ds(t * L, L), :] = to_column(v_two[t : t + 1, :])

    def third_rows(k, carry):
        rsum[pl.ds(k, 1), :] = jnp.sum(fold(am[k] * col1[...], jnp.add), axis=0, keepdims=True)
        return carry

    lax.fori_loop(0, nk, third_rows, 0, unroll=2)
    rho3[ce] = rsum[...].astype(rho3.dtype)
    cent_start(3, whole_of(rho3))
    cent_finish(3, whole_of(rho3))
    u_three = 1.0 / (n_total * added(rho3, nc))
    rp_ref[...] = (rrow[...] + jnp.log2(u_three)) * LN2


    hr = kc // 2
    cr = hr // CHUNKS
    dq = d // side
    here = (x, y)
    offsets = sorted(range(1, side), key=lambda o: -min(o, side - o))

    def along(h, stage, i):
        if (h + stage) % 2 == 0:
            return (i * side + y, ce)
        return (x * side + i, ce)

    def place(h, stage, o=0):
        return lax.rem(here[(h + stage) % 2] + o + side, side)

    def chunk(c):
        return pl.ds(c * cr, cr)

    def b1(h, c, n, to, fr):
        return pltpu.make_async_remote_copy(
            src_ref=p1s.at[h, to, chunk(c)], dst_ref=p1r.at[h, fr, chunk(c)],
            send_sem=b1s_sem.at[h, c, n], recv_sem=b1r_sem.at[h, c, n],
            device_id=along(h, 0, to), device_id_type=MESH,
        )

    def b2(h, c, n, to, fr):
        return pltpu.make_async_remote_copy(
            src_ref=p2r.at[h, fr, chunk(c)], dst_ref=p2r.at[h, fr, chunk(c)],
            send_sem=b2s_sem.at[h, c, n], recv_sem=b2r_sem.at[h, c, n],
            device_id=along(h, 1, to), device_id_type=MESH,
        )

    def out_part(h, c, i):
        return out_hbm.at[pl.ds(h * hr + c * cr, cr), pl.ds(pl.multiple_of(i * dq, L), dq)]

    def b3(h, c, n, to, fr):
        return pltpu.make_async_remote_copy(
            src_ref=p3s.at[h, chunk(c)], dst_ref=out_part(h, c, fr),
            send_sem=b3s_sem.at[h, c, n], recv_sem=b3r_sem.at[h, c, n],
            device_id=along(h, 0, to), device_id_type=MESH,
        )

    def sending(copy, stage, h, c, n):
        return copy(h, c, n, place(h, stage, offsets[n]), place(h, stage))

    def arriving(copy, stage, h, c, n):
        return copy(h, c, n, place(h, stage), place(h, stage, -offsets[n]))

    pieces = [(c, h) for c in range(CHUNKS) for h in range(2)]
    per = CHUNKS // MATS
    mr = hr // MATS

    def product_step(m, n, o):
        for h in range(2):
            i = place(h, 0, o)
            cols = pl.ds(pl.multiple_of(i * dq, L), dq)
            rows = pl.ds(m * mr, mr)
            block = jnp.dot(bm[pl.ds(h * hr + m * mr, mr), :], ev[:, cols], preferred_element_type=jnp.float32)
            block = block.astype(jnp.bfloat16)
            if n is None:
                p1r[h, i, rows] = block
            else:
                p1s[h, i, rows] = block
                for c in range(m * per, (m + 1) * per):
                    b1(h, c, n, i, place(h, 0)).start()

    for m in range(MATS):
        for h in range(2):
            for start in range(h * hr + m * mr, h * hr + (m + 1) * mr, min(SUB, mr)):
                column_block(u_three, start, min(SUB, mr), True)
        if m == MATS - 1:
            column_rows(cs3)
            dp_start(2, cs3)
        for n in range(side - 1):
            product_step(m, n, offsets[n])
        product_step(m, None, 0)

    def summed(buf, h, c):
        total = buf[h, 0, chunk(c)].astype(jnp.float32)
        for i in range(1, side):
            total = total + buf[h, i, chunk(c)].astype(jnp.float32)
        return total

    for c, h in pieces:
        for n in reversed(range(side - 1)):
            arriving(b1, 0, h, c, n).wait_recv()
        p2r[h, place(h, 1), chunk(c)] = summed(p1r, h, c).astype(jnp.bfloat16)
        for n in range(side - 1):
            sending(b2, 1, h, c, n).start()

    dp_finish(2, cs3)
    total = added(cs3, nd)
    cp_ref[...] = (crow[...] - jnp.log2(k_total * total)) * LN2
    back = 1.0 / total
    for t in range(nj):
        col1[pl.ds(t * L, L), :] = to_column(back[t : t + 1, :])

    own = []
    for c, h in pieces:
        for n in reversed(range(side - 1)):
            arriving(b2, 1, h, c, n).wait_recv()
        whole = summed(p2r, h, c)
        factor = col1[pl.ds(h * hr + c * cr, cr), :]
        for q in range(dq // L):
            p3s[h, chunk(c), q * L : (q + 1) * L] = (whole[:, q * L : (q + 1) * L] * factor).astype(jnp.bfloat16)
        for n in range(side - 1):
            sending(b3, 0, h, c, n).start()
        keep = pltpu.make_async_copy(p3s.at[h, chunk(c)], out_part(h, c, place(h, 0)), own_sem.at[h, c])
        keep.start()
        own.append(keep)

    for phase, ref in enumerate((l_part(part_a), l_part(part_b), whole_of(rho2), whole_of(rho3))):
        for k in range(nc - 1):
            cent_copy(phase, ref, k).wait_send()
    for phase, buf in enumerate((lc_all, cs2, cs3)):
        for k in range(nd - 1):
            dp_copy(phase, buf, k).wait_send()
    for c, h in pieces:
        for n in range(side - 1):
            sending(b1, 0, h, c, n).wait_send()
            sending(b2, 1, h, c, n).wait_send()
    for c, h in pieces:
        for n in reversed(range(side - 1)):
            arriving(b3, 0, h, c, n).wait_recv()
    for keep in own:
        keep.wait()
    for c, h in pieces:
        for n in range(side - 1):
            sending(b3, 0, h, c, n).wait_send()


def closing(c_in, r_in, k_in, c_out, r_out, k_out, sem):
    step = c_in.shape[0] // PIECES
    pairs = [(c_in.at[pl.ds(i * step, step)], c_out.at[pl.ds(i * step, step)]) for i in range(PIECES)]
    pairs += [(r_in, r_out), (k_in, k_out)]
    copies = [pltpu.make_async_copy(a, b, sem.at[i]) for i, (a, b) in enumerate(pairs)]
    for copy in copies:
        copy.start()
    for copy in copies:
        copy.wait()


def on_device(nd, nc, embeddings, centroids, col_start):
    rows, d = embeddings.shape
    kc = centroids.shape[0]
    side = math.isqrt(nd)
    nk, nj = rows // L, kc // L
    hr, dq = kc // 2, d // side
    f32, bf16 = jnp.float32, jnp.bfloat16
    dma = pltpu.SemaphoreType.DMA
    vmem = pl.BlockSpec(memory_space=pltpu.VMEM)
    anywhere = pl.BlockSpec(memory_space=pl.ANY)
    out, row_potential, col_potential = pl.pallas_call(
        functools.partial(kernel, nd, nc, side, float(rows * nd), float(kc * nc)),
        out_shape=(
            pltpu.VMEM((kc, d), bf16),
            pltpu.VMEM((nk, L), f32),
            pltpu.VMEM((nj, L), f32),
        ),
        in_specs=[anywhere] * 3,
        out_specs=(vmem, vmem, vmem),
        scratch_shapes=[
            pltpu.VMEM((nj, L), f32),
            pltpu.VMEM((kc, d), bf16),
            pltpu.VMEM((rows, d), bf16),
            pltpu.VMEM((nk, kc, L), f32),
            pltpu.VMEM((nk, kc, L), f32),
            pltpu.VMEM((kc, rows), bf16),
            pltpu.VMEM((kc, L), f32),
            pltpu.VMEM((kc, L), f32),
            pltpu.VMEM((kc, L), f32),
            pltpu.VMEM((nk, L), f32),
            pltpu.VMEM((nj, L), f32),
            pltpu.VMEM((nk, L), f32),
            pltpu.VMEM((nc, nk, L), f32),
            pltpu.VMEM((nc, nk, L), bf16),
            pltpu.VMEM((nc, nk, L), bf16),
            pltpu.VMEM((nd, nj, L), f32),
            pltpu.VMEM((nd, nj, L), f32),
            pltpu.VMEM((nd, nj, L), f32),
            pltpu.VMEM((2, side, hr, dq), bf16),
            pltpu.VMEM((2, side, hr, dq), bf16),
            pltpu.VMEM((2, side, hr, dq), bf16),
            pltpu.VMEM((2, hr, dq), bf16),
            dma((rows // BLK + 2,)),
            dma((4, nc - 1)),
            dma((4, nc - 1)),
            dma((3, nd - 1)),
            dma((3, nd - 1)),
            dma((2, CHUNKS, side - 1)),
            dma((2, CHUNKS, side - 1)),
            dma((2, CHUNKS, side - 1)),
            dma((2, CHUNKS, side - 1)),
            dma((2, CHUNKS, side - 1)),
            dma((2, CHUNKS, side - 1)),
            dma((2, CHUNKS)),
        ],
        compiler_params=pltpu.CompilerParams(
            collective_id=0, has_side_effects=True, vmem_limit_bytes=125 * 2**19
        ),
        cost_estimate=pl.CostEstimate(
            flops=4 * rows * kc * d, bytes_accessed=2 * (rows + 2 * kc) * d, transcendentals=2 * rows * kc
        ),
        name="sinkhorn",
    )(col_start.reshape(nj, L), centroids, embeddings)
    parts = (out, row_potential, col_potential)
    out, row_potential, col_potential = pl.pallas_call(
        closing,
        out_shape=tuple(jax.ShapeDtypeStruct(part.shape, part.dtype) for part in parts),
        in_specs=[vmem] * 3,
        out_specs=(anywhere,) * 3,
        scratch_shapes=[dma((PIECES + 2,))],
        name="closing",
    )(*(pltpu.with_memory_space_constraint(part, pltpu.VMEM) for part in parts))
    return out, row_potential.reshape(rows), col_potential.reshape(kc)


def solution(mesh):
    return jax.shard_map(
        functools.partial(on_device, mesh.shape["dp"], mesh.shape["cent"]),
        mesh=mesh,
        in_specs=(P("dp", None), P("cent", None), P("cent")),
        out_specs=(P("cent", None), P("dp"), P("cent")),
        check_vma=False,
    )
```

```python
import functools
import math

import jax
import jax.numpy as jnp
from jax import lax
from jax.experimental import pallas as pl
from jax.experimental.pallas import tpu as pltpu
from jax.sharding import PartitionSpec as P

MESH = pl.DeviceIdType.MESH
LOG2E = math.log2(math.e)
LN2 = math.log(2.0)
L = 128
BLK = 256
SUB = 128
SUB1 = 64
CHUNKS = 2
MATS = 2
PIECES = 4


def diag_mask():
    return lax.broadcasted_iota(jnp.int32, (L, L), 0) == lax.broadcasted_iota(jnp.int32, (L, L), 1)


def to_column(row):
    spread = jnp.where(diag_mask(), jnp.broadcast_to(row, (L, L)), 0.0)
    return jnp.broadcast_to(jnp.sum(spread, axis=1, keepdims=True), (L, L))


def to_row(column):
    return jnp.sum(jnp.where(diag_mask(), column, 0.0), axis=0, keepdims=True)


def fold(x, act):
    while x.shape[0] > 8:
        half = x.shape[0] // 2
        x = act(x[:half], x[half:])
    return x


def over_rows(part, rows, act):
    folded = [fold(part(pl.ds(start, SUB)), act) for start in range(0, rows, SUB)]
    total = folded[0]
    for piece in folded[1:]:
        total = act(total, piece)
    return total


def kernel(
    nd, nc, side, n_total, k_total,
    g_hbm, c_hbm, e_hbm,
    out_hbm, rp_ref, cp_ref,
    g_ref, cv, ev, tm, am, bm, gcol, col1, col2, rrow, crow, rsum,
    l_all, rho2, rho3, lc_all, cs2, cs3,
    p1s, p1r, p2r, p3s,
    load_sem, rs_sem, rr_sem, cs_sem, cr_sem,
    b1s_sem, b1r_sem, b2s_sem, b2r_sem, b3s_sem, b3r_sem, own_sem,
):
    kc, d = cv.shape
    nk = tm.shape[0]
    nb = nk * L // BLK
    nj = kc // L
    dp = lax.axis_index("dp")
    ce = lax.axis_index("cent")
    x, y = dp // side, lax.rem(dp, side)

    cent_offsets = sorted(
        ((dz, dc) for dz in range(nc // 2) for dc in range(2) if dz or dc),
        key=lambda o: (-min(o[0], nc // 2 - o[0]), o),
    )
    dp_offsets = sorted(
        ((dx, dy) for dx in range(side) for dy in range(side) if dx or dy),
        key=lambda o: (-min(o[0], side - o[0]) - min(o[1], side - o[1]), o),
    )
    z, core = ce // 2, lax.rem(ce, 2)

    def cent_at(o, sign):
        return lax.rem(z + sign * o[0] + nc // 2, nc // 2) * 2 + lax.rem(core + o[1], 2)

    def dp_at(o, sign):
        return lax.rem(x + sign * o[0] + side, side) * side + lax.rem(y + sign * o[1] + side, side)

    c_load = pltpu.make_async_copy(c_hbm, cv, load_sem.at[nb])
    g_load = pltpu.make_async_copy(g_hbm, g_ref, load_sem.at[nb + 1])
    c_load.start()
    g_load.start()

    def e_load(b):
        rows = pl.ds(b * BLK, BLK)
        return pltpu.make_async_copy(e_hbm.at[rows], ev.at[rows], load_sem.at[b])

    for b in range(nb):
        e_load(b).start()

    barrier = pltpu.get_barrier_semaphore()
    for o in cent_offsets:
        pl.semaphore_signal(barrier, inc=1, device_id=(dp, cent_at(o, 1)), device_id_type=MESH)
    for o in dp_offsets:
        pl.semaphore_signal(barrier, inc=1, device_id=(dp_at(o, 1), ce), device_id_type=MESH)

    g_load.wait()
    for t in range(nj):
        gcol[pl.ds(t * L, L), :] = to_column(g_ref[pl.ds(t, 1), :] * LOG2E)
    c_load.wait()

    scale = LOG2E / math.sqrt(d)

    def score_block(b, carry):
        e_load(b).wait()
        block = ev[pl.ds(pl.multiple_of(b * BLK, BLK), BLK), :]
        product = lax.dot_general(cv[...], block, (((1,), (1,)), ((), ())), preferred_element_type=jnp.float32)
        product = product * scale
        for h in range(BLK // L):
            tm[b * (BLK // L) + h] = product[:, h * L : (h + 1) * L]
        for h in range(BLK // L):
            k = b * (BLK // L) + h
            peak = jnp.max(over_rows(lambda r: tm[k, r, :] + gcol[r, :], kc, jnp.maximum), axis=0, keepdims=True)
            mass = jnp.sum(over_rows(lambda r: jnp.exp2(tm[k, r, :] + gcol[r, :] - peak), kc, jnp.add), axis=0, keepdims=True)
            l_all[ce, pl.ds(k, 1), :] = peak + jnp.log2(mass)
        return carry

    def cent_copy(phase, ref, k):
        return pltpu.make_async_remote_copy(
            src_ref=ref(ce), dst_ref=ref(ce),
            send_sem=rs_sem.at[phase, k], recv_sem=rr_sem.at[phase, k],
            device_id=(dp, cent_at(cent_offsets[k], 1)), device_id_type=MESH,
        )

    def cent_arrival(phase, ref, k):
        fr = cent_at(cent_offsets[k], -1)
        return pltpu.make_async_remote_copy(
            src_ref=ref(fr), dst_ref=ref(fr),
            send_sem=rs_sem.at[phase, k], recv_sem=rr_sem.at[phase, k],
            device_id=(dp, fr), device_id_type=MESH,
        )

    def dp_copy(phase, buf, k):
        return pltpu.make_async_remote_copy(
            src_ref=buf.at[dp], dst_ref=buf.at[dp],
            send_sem=cs_sem.at[phase, k], recv_sem=cr_sem.at[phase, k],
            device_id=(dp_at(dp_offsets[k], 1), ce), device_id_type=MESH,
        )

    def dp_arrival(phase, buf, k):
        fr = dp_at(dp_offsets[k], -1)
        return pltpu.make_async_remote_copy(
            src_ref=buf.at[fr], dst_ref=buf.at[fr],
            send_sem=cs_sem.at[phase, k], recv_sem=cr_sem.at[phase, k],
            device_id=(fr, ce), device_id_type=MESH,
        )

    def cent_start(phase, ref):
        for k in range(nc - 1):
            cent_copy(phase, ref, k).start()

    def cent_finish(phase, ref):
        for k in reversed(range(nc - 1)):
            cent_arrival(phase, ref, k).wait_recv()

    def dp_start(phase, buf):
        for k in range(nd - 1):
            dp_copy(phase, buf, k).start()

    def dp_finish(phase, buf):
        for k in reversed(range(nd - 1)):
            dp_arrival(phase, buf, k).wait_recv()

    early = nk // 2
    part_a = pl.ds(0, early)
    part_b = pl.ds(early, nk - early)

    def l_part(part):
        return lambda s: l_all.at[s, part]

    def whole_of(buf):
        return lambda s: buf.at[s]

    def joined(buf, n):
        peak = buf[0]
        for s in range(1, n):
            peak = jnp.maximum(peak, buf[s])
        total = jnp.exp2(buf[0] - peak)
        for s in range(1, n):
            total = total + jnp.exp2(buf[s] - peak)
        return peak + jnp.log2(total)

    def added(buf, n):
        total = buf[0].astype(jnp.float32)
        for s in range(1, n):
            total = total + buf[s].astype(jnp.float32)
        return total

    lax.fori_loop(0, early * L // BLK, score_block, 0)
    pl.semaphore_wait(barrier, nc - 1 + nd - 1)
    cent_start(0, l_part(part_a))
    lax.fori_loop(early * L // BLK, nb, score_block, 0)
    cent_start(1, l_part(part_b))
    cent_finish(0, l_part(part_a))
    cent_finish(1, l_part(part_b))

    rrow[...] = -math.log2(n_total) - joined(l_all, nc)

    def first_columns(jb, carry):
        rows = pl.ds(pl.multiple_of(jb * SUB1, SUB1), SUB1)
        peak = tm[0, rows, :] + rrow[pl.ds(0, 1), :]
        for k in range(1, nk):
            peak = jnp.maximum(peak, tm[k, rows, :] + rrow[pl.ds(k, 1), :])
        peak = jnp.broadcast_to(jnp.max(peak, axis=1, keepdims=True), (SUB1, L))
        mass = jnp.zeros((SUB1, L), jnp.float32)
        for k in range(nk):
            value = jnp.exp2(tm[k, rows, :] + rrow[pl.ds(k, 1), :] - peak)
            am[k, rows, :] = value
            mass = mass + value
        col1[rows, :] = peak
        col2[rows, :] = jnp.broadcast_to(jnp.sum(mass, axis=1, keepdims=True), (SUB1, L))
        return carry

    lax.fori_loop(0, kc // SUB1, first_columns, 0, unroll=2)
    for t in range(nj):
        top = to_row(col1[pl.ds(t * L, L), :])
        crow[pl.ds(t, 1), :] = top
        lc_all[dp, pl.ds(t, 1), :] = top + jnp.log2(to_row(col2[pl.ds(t * L, L), :]))
    dp_start(0, lc_all)
    dp_finish(0, lc_all)
    g_one = -math.log2(k_total) - joined(lc_all, nd)
    lift = jnp.exp2(crow[...] + g_one)
    crow[...] = g_one
    for t in range(nj):
        col1[pl.ds(t * L, L), :] = to_column(lift[t : t + 1, :])

    def second_rows(k, carry):
        def lifted(r):
            value = am[k, r, :] * col1[r, :]
            am[k, r, :] = value
            return value

        rsum[pl.ds(k, 1), :] = jnp.sum(over_rows(lifted, kc, jnp.add), axis=0, keepdims=True)
        return carry

    lax.fori_loop(0, nk, second_rows, 0, unroll=2)
    rho2[ce] = rsum[...].astype(rho2.dtype)
    cent_start(2, whole_of(rho2))
    cent_finish(2, whole_of(rho2))
    u_two = 1.0 / (n_total * added(rho2, nc))

    def column_block(u, start, size, keep):
        rows = pl.ds(start, size)
        mass = jnp.zeros((size, L), jnp.float32)
        for k in range(nk):
            value = am[k, rows, :] * u[k : k + 1, :]
            if keep:
                bm[rows, k * L : (k + 1) * L] = value.astype(jnp.bfloat16)
            mass = mass + value
        col2[rows, :] = jnp.broadcast_to(jnp.sum(mass, axis=1, keepdims=True), (size, L))

    def column_rows(target):
        for t in range(nj):
            target[dp, pl.ds(t, 1), :] = to_row(col2[pl.ds(t * L, L), :])

    for start in range(0, kc, SUB):
        column_block(u_two, start, SUB, False)
    column_rows(cs2)
    dp_start(1, cs2)
    dp_finish(1, cs2)
    v_two = 1.0 / (k_total * added(cs2, nd))
    for t in range(nj):
        col1[pl.ds(t * L, L), :] = to_column(v_two[t : t + 1, :])

    def third_rows(k, carry):
        rho3[ce, pl.ds(k, 1), :] = jnp.sum(over_rows(lambda r: am[k, r, :] * col1[r, :], kc, jnp.add), axis=0, keepdims=True)
        return carry

    lax.fori_loop(0, nk, third_rows, 0, unroll=2)
    cent_start(3, whole_of(rho3))
    cent_finish(3, whole_of(rho3))
    u_three = 1.0 / (n_total * added(rho3, nc))
    rp_ref[...] = (rrow[...] + jnp.log2(u_three)) * LN2


    hr = kc // 2
    cr = hr // CHUNKS
    dq = d // side
    here = (x, y)
    offsets = sorted(range(1, side), key=lambda o: -min(o, side - o))

    def along(h, stage, i):
        if (h + stage) % 2 == 0:
            return (i * side + y, ce)
        return (x * side + i, ce)

    def place(h, stage, o=0):
        return lax.rem(here[(h + stage) % 2] + o + side, side)

    def chunk(c):
        return pl.ds(c * cr, cr)

    def b1(h, c, n, to, fr):
        return pltpu.make_async_remote_copy(
            src_ref=p1s.at[h, to, chunk(c)], dst_ref=p1r.at[h, fr, chunk(c)],
            send_sem=b1s_sem.at[h, c, n], recv_sem=b1r_sem.at[h, c, n],
            device_id=along(h, 0, to), device_id_type=MESH,
        )

    def b2(h, c, n, to, fr):
        return pltpu.make_async_remote_copy(
            src_ref=p2r.at[h, fr, chunk(c)], dst_ref=p2r.at[h, fr, chunk(c)],
            send_sem=b2s_sem.at[h, c, n], recv_sem=b2r_sem.at[h, c, n],
            device_id=along(h, 1, to), device_id_type=MESH,
        )

    def out_part(h, c, i):
        return out_hbm.at[pl.ds(h * hr + c * cr, cr), pl.ds(pl.multiple_of(i * dq, L), dq)]

    def b3(h, c, n, to, fr):
        return pltpu.make_async_remote_copy(
            src_ref=p3s.at[h, chunk(c)], dst_ref=out_part(h, c, fr),
            send_sem=b3s_sem.at[h, c, n], recv_sem=b3r_sem.at[h, c, n],
            device_id=along(h, 0, to), device_id_type=MESH,
        )

    def sending(copy, stage, h, c, n):
        return copy(h, c, n, place(h, stage, offsets[n]), place(h, stage))

    def arriving(copy, stage, h, c, n):
        return copy(h, c, n, place(h, stage), place(h, stage, -offsets[n]))

    pieces = [(c, h) for c in range(CHUNKS) for h in range(2)]
    per = CHUNKS // MATS
    mr = hr // MATS

    def product_step(m, n, o):
        for h in range(2):
            i = place(h, 0, o)
            cols = pl.ds(pl.multiple_of(i * dq, L), dq)
            rows = pl.ds(m * mr, mr)
            block = jnp.dot(bm[pl.ds(h * hr + m * mr, mr), :], ev[:, cols], preferred_element_type=jnp.float32)
            block = block.astype(jnp.bfloat16)
            if n is None:
                p1r[h, i, rows] = block
            else:
                p1s[h, i, rows] = block
                for c in range(m * per, (m + 1) * per):
                    b1(h, c, n, i, place(h, 0)).start()

    for m in range(MATS):
        for h in range(2):
            for start in range(h * hr + m * mr, h * hr + (m + 1) * mr, min(SUB, mr)):
                column_block(u_three, start, min(SUB, mr), True)
        if m == MATS - 1:
            column_rows(cs3)
            dp_start(2, cs3)
        for n in range(side - 1):
            product_step(m, n, offsets[n])
        product_step(m, None, 0)

    def summed(buf, h, c):
        total = buf[h, 0, chunk(c)].astype(jnp.float32)
        for i in range(1, side):
            total = total + buf[h, i, chunk(c)].astype(jnp.float32)
        return total

    for c, h in pieces:
        for n in reversed(range(side - 1)):
            arriving(b1, 0, h, c, n).wait_recv()
        p2r[h, place(h, 1), chunk(c)] = summed(p1r, h, c).astype(jnp.bfloat16)
        for n in range(side - 1):
            sending(b2, 1, h, c, n).start()

    dp_finish(2, cs3)
    total = added(cs3, nd)
    cp_ref[...] = (crow[...] - jnp.log2(k_total * total)) * LN2
    back = 1.0 / total
    for t in range(nj):
        col1[pl.ds(t * L, L), :] = to_column(back[t : t + 1, :])

    own = []
    for c, h in pieces:
        for n in reversed(range(side - 1)):
            arriving(b2, 1, h, c, n).wait_recv()
        whole = summed(p2r, h, c)
        factor = col1[pl.ds(h * hr + c * cr, cr), :]
        for q in range(dq // L):
            p3s[h, chunk(c), q * L : (q + 1) * L] = (whole[:, q * L : (q + 1) * L] * factor).astype(jnp.bfloat16)
        for n in range(side - 1):
            sending(b3, 0, h, c, n).start()
        keep = pltpu.make_async_copy(p3s.at[h, chunk(c)], out_part(h, c, place(h, 0)), own_sem.at[h, c])
        keep.start()
        own.append(keep)

    for phase, ref in enumerate((l_part(part_a), l_part(part_b), whole_of(rho2), whole_of(rho3))):
        for k in range(nc - 1):
            cent_copy(phase, ref, k).wait_send()
    for phase, buf in enumerate((lc_all, cs2, cs3)):
        for k in range(nd - 1):
            dp_copy(phase, buf, k).wait_send()
    for c, h in pieces:
        for n in range(side - 1):
            sending(b1, 0, h, c, n).wait_send()
            sending(b2, 1, h, c, n).wait_send()
    for c, h in pieces:
        for n in reversed(range(side - 1)):
            arriving(b3, 0, h, c, n).wait_recv()
    for keep in own:
        keep.wait()
    for c, h in pieces:
        for n in range(side - 1):
            sending(b3, 0, h, c, n).wait_send()


def closing(c_in, r_in, k_in, c_out, r_out, k_out, sem):
    step = c_in.shape[0] // PIECES
    pairs = [(c_in.at[pl.ds(i * step, step)], c_out.at[pl.ds(i * step, step)]) for i in range(PIECES)]
    pairs += [(r_in, r_out), (k_in, k_out)]
    copies = [pltpu.make_async_copy(a, b, sem.at[i]) for i, (a, b) in enumerate(pairs)]
    for copy in copies:
        copy.start()
    for copy in copies:
        copy.wait()


def on_device(nd, nc, embeddings, centroids, col_start):
    rows, d = embeddings.shape
    kc = centroids.shape[0]
    side = math.isqrt(nd)
    nk, nj = rows // L, kc // L
    hr, dq = kc // 2, d // side
    f32, bf16 = jnp.float32, jnp.bfloat16
    dma = pltpu.SemaphoreType.DMA
    vmem = pl.BlockSpec(memory_space=pltpu.VMEM)
    anywhere = pl.BlockSpec(memory_space=pl.ANY)
    out, row_potential, col_potential = pl.pallas_call(
        functools.partial(kernel, nd, nc, side, float(rows * nd), float(kc * nc)),
        out_shape=(
            pltpu.VMEM((kc, d), bf16),
            pltpu.VMEM((nk, L), f32),
            pltpu.VMEM((nj, L), f32),
        ),
        in_specs=[anywhere] * 3,
        out_specs=(vmem, vmem, vmem),
        scratch_shapes=[
            pltpu.VMEM((nj, L), f32),
            pltpu.VMEM((kc, d), bf16),
            pltpu.VMEM((rows, d), bf16),
            pltpu.VMEM((nk, kc, L), f32),
            pltpu.VMEM((nk, kc, L), f32),
            pltpu.VMEM((kc, rows), bf16),
            pltpu.VMEM((kc, L), f32),
            pltpu.VMEM((kc, L), f32),
            pltpu.VMEM((kc, L), f32),
            pltpu.VMEM((nk, L), f32),
            pltpu.VMEM((nj, L), f32),
            pltpu.VMEM((nk, L), f32),
            pltpu.VMEM((nc, nk, L), f32),
            pltpu.VMEM((nc, nk, L), bf16),
            pltpu.VMEM((nc, nk, L), f32),
            pltpu.VMEM((nd, nj, L), f32),
            pltpu.VMEM((nd, nj, L), f32),
            pltpu.VMEM((nd, nj, L), f32),
            pltpu.VMEM((2, side, hr, dq), bf16),
            pltpu.VMEM((2, side, hr, dq), bf16),
            pltpu.VMEM((2, side, hr, dq), bf16),
            pltpu.VMEM((2, hr, dq), bf16),
            dma((rows // BLK + 2,)),
            dma((4, nc - 1)),
            dma((4, nc - 1)),
            dma((3, nd - 1)),
            dma((3, nd - 1)),
            dma((2, CHUNKS, side - 1)),
            dma((2, CHUNKS, side - 1)),
            dma((2, CHUNKS, side - 1)),
            dma((2, CHUNKS, side - 1)),
            dma((2, CHUNKS, side - 1)),
            dma((2, CHUNKS, side - 1)),
            dma((2, CHUNKS)),
        ],
        compiler_params=pltpu.CompilerParams(
            collective_id=0, has_side_effects=True, vmem_limit_bytes=125 * 2**19
        ),
        cost_estimate=pl.CostEstimate(
            flops=4 * rows * kc * d, bytes_accessed=2 * (rows + 2 * kc) * d, transcendentals=2 * rows * kc
        ),
        name="sinkhorn",
    )(col_start.reshape(nj, L), centroids, embeddings)
    parts = (out, row_potential, col_potential)
    out, row_potential, col_potential = pl.pallas_call(
        closing,
        out_shape=tuple(jax.ShapeDtypeStruct(part.shape, part.dtype) for part in parts),
        in_specs=[vmem] * 3,
        out_specs=(anywhere,) * 3,
        scratch_shapes=[dma((PIECES + 2,))],
        name="closing",
    )(*(pltpu.with_memory_space_constraint(part, pltpu.VMEM) for part in parts))
    return out, row_potential.reshape(rows), col_potential.reshape(kc)


def solution(mesh):
    return jax.shard_map(
        functools.partial(on_device, mesh.shape["dp"], mesh.shape["cent"]),
        mesh=mesh,
        in_specs=(P("dp", None), P("cent", None), P("cent")),
        out_specs=(P("cent", None), P("dp"), P("cent")),
        check_vma=False,
    )
```
